1024 devices in a mesh: row: 128 (over z, y), col: 8 (over x, core).
Axes of the slice: x: 4, y: 8, z: 16, core: 2. Of those that a mesh axis runs over, the one named last changes fastest.
Arguments:
- features: bfloat16 [65536, 512], P('row', 'col'), may hold values from -6 to 6
- adjacency: bfloat16 [65536, 5, 512], P('row'), may hold values from 0 to 1, as said below
- tile_mask: int32 [512, 5, 4], P('row'), may hold values from 0 to 1, as said below
- w_self: bfloat16 [512, 512], P('col'), may hold values from -0.25 to 0.25
- w_neigh: bfloat16 [512, 512], P('col'), may hold values from -0.25 to 0.25
- cotangent: bfloat16 [65536, 512], P('row', 'col'), may hold values from -6 to 6
Outputs:
- activated: bfloat16 [65536, 512], P('row', 'col')
- grad_features: bfloat16 [65536, 512], P('row', 'col')
- grad_self: float32 [512, 512], P('col')
- grad_neigh: float32 [512, 512], P('col')
The draws below stay inside these ranges and needn't reach their ends.
Inputs may be any that keep to these rules, and one draw needn't show every extreme that they name: `adjacency`: edge weights. Each node has at most 24 edges; every edge links to a node near the node's own position within its panel, in its own panel or in one up to 2 panels away. `tile_mask`: exactly the tiles that hold an edge are marked 1; how many varies from panel to panel.
All inputs are finite; a program needn't handle non-finite values.
Results may differ from the reference program's by a relative error of at most 0.0052.
Values may be sent and summed in bfloat16 or wider, within the bound.
No kernel may reach another device: no remote copies, remote signals or barrier semaphores. Data moves between devices by JAX's collectives and lax.ppermute only.
A program may use at most 32 MiB of HBM per device.

```python
import math
import jax
import jax.numpy as jnp
from jax import lax

F = 512
NODE_DEV = 512
BAND = 2
BANDS = 5
NODES = 65536


def edge_layout(key):
    slot_count = 24
    panel_count = NODES // NODE_DEV
    count_key, reach_key, band_key, shift_key, open_key = jax.random.split(jax.random.fold_in(key, 5), 5)
    edge_count = jax.random.randint(count_key, (panel_count,), 2, slot_count + 1)
    reach = jax.random.randint(reach_key, (panel_count,), 16, 129)
    node_ids = jnp.arange(NODES, dtype=jnp.int32)
    panel_of = node_ids // NODE_DEV
    local_of = node_ids % NODE_DEV
    roll = jax.random.randint(band_key, (NODES, slot_count), 0, 20)
    band_pick = jnp.where(roll < 8, BAND, jnp.where(roll < 11, BAND - 1, jnp.where(roll < 14, BAND + 1, jnp.where(roll < 17, BAND - 2, BAND + 2))))
    band_pick = band_pick.astype(jnp.int32)
    opened = (jax.random.randint(open_key, (NODES // 128, BANDS), 0, 5) < 3).astype(jnp.int32)
    band_ids = jnp.arange(BANDS, dtype=jnp.int32)[None, :]
    opened = jnp.where(band_ids == BAND, 1, opened).astype(jnp.int32)
    tile_open = jnp.take_along_axis(opened[node_ids // 128], band_pick, axis=1)
    band_pick = jnp.where(tile_open > 0, band_pick, BAND).astype(jnp.int32)
    node_reach = reach[panel_of][:, None]
    unit = jax.random.randint(shift_key, (NODES, slot_count), 0, 1 << 20)
    offset_col = unit % (2 * node_reach + 1) - node_reach
    column = jnp.clip(local_of[:, None] + offset_col, 0, NODE_DEV - 1).astype(jnp.int32)
    slot_ids = jnp.arange(slot_count, dtype=jnp.int32)[None, :]
    active = (slot_ids < edge_count[panel_of][:, None]).astype(jnp.int32)
    return (node_ids, band_pick, column, active)


def draw_adjacency(key, part):
    node_ids, band_pick, column, active = edge_layout(key)
    key = jax.random.fold_in(key, 11)
    weights = jax.random.uniform(key, column.shape, jnp.float32, 0.05, 1.0)
    weights = weights * active.astype(jnp.float32)
    flat = (node_ids[:, None] * BANDS + band_pick) * NODE_DEV + column
    dense = jnp.zeros((NODES * BANDS * NODE_DEV,), jnp.float32).at[flat.reshape(-1)].max(weights.reshape(-1))
    return dense.reshape(NODES, BANDS, NODE_DEV).astype(jnp.bfloat16)


def draw_tile_mask(key, part):
    node_ids, band_pick, column, active = edge_layout(key)
    tile_side = NODE_DEV // 128
    flat = (node_ids[:, None] // 128 * BANDS + band_pick) * tile_side + column // 128
    grid = jnp.zeros((NODES // 128 * BANDS * tile_side,), jnp.int32).at[flat.reshape(-1)].max(active.reshape(-1))
    return grid.reshape(NODES // 128, BANDS, tile_side)


def level_of(own_key, shape, cuts, low, high):
    def one(dim, parts):
        heights = jax.random.uniform(jax.random.fold_in(jax.random.fold_in(own_key, 6), dim), (parts,), jnp.float32, low / len(cuts), high / len(cuts))
        return jnp.repeat(jnp.exp(heights), shape[dim] // parts).reshape((-1,) + (1,) * (len(shape) - dim - 1))

    loudness = one(*cuts[0])
    for cut in cuts[1:]:
        loudness = loudness * one(*cut)
    return loudness


def gaussian(own_key, dims, scale, most, pieces=(), kind=jnp.bfloat16):
    drawn = scale * jax.random.normal(own_key, dims, jnp.float32)
    if pieces:
        drawn = drawn * level_of(own_key, dims, pieces, -0.22, 0.18)
    return jnp.clip(drawn, -most, most).astype(kind)


def setup_inputs(seed: int = 0) -> dict:
    streams_of = jax.random.split(jax.random.key(seed), 7)
    return {
        "features": gaussian(streams_of[0], (NODES, F), 1.0, 6.0, ((0, 128), (1, 8))),
        "adjacency": draw_adjacency(jax.random.fold_in(streams_of[6], 71), 0),
        "tile_mask": draw_tile_mask(jax.random.fold_in(streams_of[6], 71), 0),
        "w_self": gaussian(streams_of[3], (F, F), F ** -0.5, 0.25, ((0, 8),)),
        "w_neigh": gaussian(streams_of[4], (F, F), F ** -0.5, 0.25, ((0, 8),)),
        "cotangent": gaussian(streams_of[5], (NODES, F), 1.0, 6.0, ((0, 128), (1, 8))),
    }


def masked_band(adj_block, mask_block):
    tile_rows = mask_block.shape[0]
    band_count = mask_block.shape[1]
    tile_cols = mask_block.shape[2]
    blocks = adj_block.reshape(tile_rows, 128, band_count, tile_cols, 128)
    tile_keep = mask_block.astype(jnp.bfloat16)[:, None, :, :, None]
    return (blocks * tile_keep).reshape(adj_block.shape)

def reference(features, adjacency, tile_mask, w_self, w_neigh, cotangent):
    panel_count = NODES // NODE_DEV
    band_count = 2 * BAND + 1
    tile_side = NODE_DEV // 128
    feat_panels = features.reshape(panel_count, NODE_DEV, F)
    adj_panels = adjacency.reshape(panel_count, NODE_DEV, band_count, NODE_DEV)
    mask_panels = tile_mask.reshape(panel_count, tile_side, band_count, tile_side)
    offsets = jnp.arange(band_count, dtype=jnp.int32) - BAND
    panel_ids = jnp.arange(panel_count, dtype=jnp.int32)

    def forward_panel(panel):
        weighted = masked_band(adj_panels[panel], mask_panels[panel]).astype(jnp.float32)
        source_panels = (panel + offsets) % panel_count
        band_feat = feat_panels[source_panels].astype(jnp.float32)
        summed = jnp.einsum('rjc,jcf->rf', weighted, band_feat)
        degree = lax.optimization_barrier(jnp.sum(weighted, axis=(1, 2)))
        return (summed, degree)
    summed, degree = lax.map(forward_panel, panel_ids)
    inverse = 1.0 / jnp.maximum(degree, 1.0)
    mean_neigh = (summed * inverse[..., None]).astype(jnp.bfloat16).reshape(NODES, F)
    preact = jnp.dot(features, w_self, preferred_element_type=jnp.float32)
    preact = preact + jnp.dot(mean_neigh, w_neigh, preferred_element_type=jnp.float32)
    sigmoid_z = jax.nn.sigmoid(preact)
    activated = (preact * sigmoid_z).astype(jnp.bfloat16)
    slope = sigmoid_z * (1.0 + preact * (1.0 - sigmoid_z))
    grad_preact = (cotangent.astype(jnp.float32) * slope).astype(jnp.bfloat16)
    self_part = jnp.dot(grad_preact, w_self.T, preferred_element_type=jnp.float32)
    neigh_part = jnp.dot(grad_preact, w_neigh.T, preferred_element_type=jnp.float32)
    spread = (neigh_part.reshape(panel_count, NODE_DEV, F) * inverse[..., None]).astype(jnp.bfloat16)
    band_ids = jnp.arange(band_count, dtype=jnp.int32)

    def backward_panel(panel):
        senders = (panel - offsets) % panel_count
        blocks = adj_panels[senders, :, band_ids, :]
        mask_sel = mask_panels[senders, :, band_ids, :]
        tile_keep = mask_sel.astype(jnp.bfloat16)[:, :, None, :, None]
        blocks = blocks.reshape(band_count, tile_side, 128, tile_side, 128) * tile_keep
        blocks = blocks.reshape(band_count, NODE_DEV, NODE_DEV).astype(jnp.float32)
        return jnp.einsum('jrc,jrf->cf', blocks, spread[senders].astype(jnp.float32))
    returned = lax.map(backward_panel, panel_ids).reshape(NODES, F)
    grad_features = (self_part + returned).astype(jnp.bfloat16)
    grad_scale = 1.0 / math.sqrt(NODES)
    grad_self = jnp.dot(features.T, grad_preact, preferred_element_type=jnp.float32) * grad_scale
    grad_neigh = jnp.dot(mean_neigh.T, grad_preact, preferred_element_type=jnp.float32) * grad_scale
    return (activated, grad_features, grad_self, grad_neigh)
```

```python
import math

import jax
import jax.numpy as jnp
from jax import lax
from jax.experimental import pallas as pl
from jax.experimental.pallas import tpu as pltpu
from jax.sharding import Mesh
from jax.sharding import PartitionSpec as P

ROW = ("z", "y")
COL = ("x", "core")
TILE = 128
DOT = dict(preferred_element_type=jnp.float32)


def mask_kernel(mask_ref, adj_ref, out_ref):
    band = pl.program_id(0)
    for row in range(adj_ref.shape[1] // TILE):
        for column in range(adj_ref.shape[2] // TILE):
            rows = pl.ds(row * TILE, TILE)
            columns = pl.ds(column * TILE, TILE)
            keep = mask_ref[row, band, column].astype(jnp.float32).astype(jnp.bfloat16)
            out_ref[0, rows, columns] = adj_ref[0, rows, columns] * keep


def masked_bands(bands, mask):
    count, rows, columns = bands.shape
    block = pl.BlockSpec((1, rows, columns), lambda band: (band, 0, 0))
    return pl.pallas_call(
        mask_kernel,
        grid=(count,),
        out_shape=jax.ShapeDtypeStruct(bands.shape, bands.dtype),
        in_specs=[pl.BlockSpec(memory_space=pltpu.SMEM), block],
        out_specs=block,
        cost_estimate=pl.CostEstimate(
            flops=bands.size, bytes_accessed=4 * bands.size, transcendentals=0
        ),
    )(mask, bands)


def from_behind(value, steps):
    count = lax.axis_size(ROW)
    pairs = [(source, (source + steps) % count) for source in range(count)]
    return lax.ppermute(value, ROW, pairs)


def exchange(chunks, axes):
    return lax.all_to_all(chunks, axes, 0, 0, tiled=True)


def to_all(value, axes):
    copies = jnp.broadcast_to(value, (lax.axis_size(axes),) + value.shape)
    return exchange(copies, axes)


def body(features, adjacency, tile_mask, w_self, w_neigh, cotangent):
    own = features.T
    width, nodes = own.shape
    groups = lax.axis_size(COL)
    lines = lax.axis_size("y")
    total = groups * width
    band_reach = (tile_mask.shape[1] - 1) // 2
    offsets = [k for k in range(-band_reach, band_reach + 1) if k != 0]

    columns_out = jnp.concatenate(
        [
            jnp.broadcast_to(own, (groups, width, nodes)),
            w_self.reshape(width, groups, width).transpose(1, 0, 2),
            w_neigh.reshape(width, groups, width).transpose(1, 0, 2),
        ],
        axis=2,
    )
    neighbours = {k: from_behind(own, -k) for k in offsets}
    early = exchange(columns_out, COL)
    feats = early[:, :, :nodes]
    self_cols = early[:, :, nodes : nodes + width].reshape(total, width)
    neigh_cols = early[:, :, nodes + width :].reshape(total, width)

    weighted = masked_bands(adjacency.transpose(1, 0, 2), tile_mask)
    degree = jnp.sum(weighted, axis=(0, 2), dtype=jnp.float32)
    inverse = 1.0 / jnp.maximum(degree, 1.0)
    last = (((1,), (1,)), ((), ()))
    first = (((0,), (0,)), ((), ()))
    summed = lax.dot_general(own, weighted[band_reach], last, **DOT)
    for k in offsets:
        summed = summed + lax.dot_general(neighbours[k], weighted[band_reach + k], last, **DOT)
    mean = (summed * inverse[None, :]).astype(jnp.bfloat16)
    means = to_all(mean, COL)

    preact = lax.dot_general(self_cols, feats.reshape(total, nodes), first, **DOT)
    preact = preact + lax.dot_general(neigh_cols, means.reshape(total, nodes), first, **DOT)
    sigmoid_z = jax.nn.sigmoid(preact)
    activated = (preact * sigmoid_z).astype(jnp.bfloat16)
    slope = sigmoid_z * (1.0 + preact * (1.0 - sigmoid_z))
    grad_preact = (cotangent.T.astype(jnp.float32) * slope).astype(jnp.bfloat16)

    grad_scale = 1.0 / math.sqrt(lax.axis_size(ROW) * nodes)
    stacked = jnp.concatenate([feats, means], axis=1).reshape(2 * total, nodes)
    partial = lax.dot_general(grad_preact, stacked, last, **DOT) * grad_scale
    pieces = partial.astype(jnp.bfloat16).reshape(lines, width // lines, 2 * total)
    over_y = jnp.sum(exchange(pieces, "y").astype(jnp.float32), axis=0)
    over_z = jnp.sum(to_all(over_y.astype(jnp.bfloat16), "z").astype(jnp.float32), axis=0)
    shares = over_z.reshape(width // lines, groups, 2 * width).transpose(1, 0, 2)
    shares = jnp.broadcast_to(shares[:, None], (groups, lines) + shares.shape[1:])
    shares = shares.reshape((groups * lines,) + shares.shape[2:])
    gathered = exchange(shares, COL + ("y",)).reshape(total, 2 * width).T

    grads = to_all(grad_preact, COL).reshape(total, nodes)
    spread = (jnp.dot(w_neigh, grads, **DOT) * inverse[None, :]).astype(jnp.bfloat16)
    terms = {
        k: jnp.dot(spread, weighted[band_reach + k], **DOT).astype(jnp.bfloat16) for k in offsets
    }
    returned = jnp.dot(w_self, grads, **DOT) + jnp.dot(spread, weighted[band_reach], **DOT)
    for k in offsets:
        returned = returned + from_behind(terms[k], k).astype(jnp.float32)
    grad_features = returned.astype(jnp.bfloat16)
    return (activated.T, grad_features.T, gathered[:width], gathered[width:])


def solution(mesh):
    rows, columns = mesh.devices.shape
    lines = math.gcd(rows, 8)
    cores = math.gcd(columns, 2)
    fine = Mesh(
        mesh.devices.reshape(rows // lines, lines, columns // cores, cores), ROW + COL
    )
    return jax.shard_map(
        body,
        mesh=fine,
        in_specs=(
            P(ROW, COL),
            P(ROW, None, None),
            P(ROW, None, None),
            P(COL, None),
            P(COL, None),
            P(ROW, COL),
        ),
        out_specs=(P(ROW, COL), P(ROW, COL), P(COL, None), P(COL, None)),
        check_vma=False,
    )
```

```python
import math

import jax
import jax.numpy as jnp
from jax import lax
from jax.experimental import pallas as pl
from jax.experimental.pallas import tpu as pltpu
from jax.sharding import Mesh
from jax.sharding import PartitionSpec as P

ROW = ("z", "y")
COL = ("x", "core")
TILE = 128
LAST = (((1,), (1,)), ((), ()))
FIRST = (((0,), (0,)), ((), ()))
PLAIN = (((1,), (0,)), ((), ()))
VMEM = pl.BlockSpec(memory_space=pltpu.VMEM)
SMEM = pl.BlockSpec(memory_space=pltpu.SMEM)
ANY = pl.BlockSpec(memory_space=pl.ANY)
BF16 = jnp.bfloat16
F32 = jnp.float32


def fetch(sources, buffer, arrived):
    copies = [
        pltpu.make_async_copy(source, buffer.at[slot], arrived.at[slot])
        for slot, source in enumerate(sources)
    ]
    for copy in copies:
        copy.start()
    return copies


def slots(count, shape):
    return [pltpu.VMEM((count, *shape), BF16), pltpu.SemaphoreType.DMA((count,))]


def dot(a, b, dims):
    return lax.dot_general(a, b, dims, preferred_element_type=F32)


def local_call(kernel, out_shape, in_specs, args, flops, scratch=()):
    outs = jax.tree.leaves(out_shape)
    moved = sum(a.size * a.dtype.itemsize for a in (*args, *outs))
    return pl.pallas_call(
        kernel,
        out_shape=out_shape,
        in_specs=in_specs,
        out_specs=jax.tree.map(lambda _: VMEM, out_shape),
        scratch_shapes=list(scratch),
        compiler_params=pltpu.CompilerParams(vmem_limit_bytes=24 * 1024 * 1024),
        cost_estimate=pl.CostEstimate(flops=flops, bytes_accessed=moved, transcendentals=0),
    )(*args)


def prep_kernel(own_ref, wself_ref, wneigh_ref, out_ref, buffer, arrived):
    groups, width, _ = out_ref.shape
    nodes = own_ref.shape[1]
    for copy in fetch((own_ref, wself_ref, wneigh_ref), buffer, arrived):
        copy.wait()
    own, wself, wneigh = buffer[0], buffer[1], buffer[2]
    for group in range(groups):
        out_ref[group, :, :nodes] = own
        columns = slice(group * width, (group + 1) * width)
        out_ref[group, :, nodes:] = jnp.concatenate([wself[:, columns], wneigh[:, columns]], axis=1)


def mask_kernel(
    mask_ref, own_ref, adj_ref, _, weighted_ref, base_ref, inverse_ref, buffer, arrived, near, here
):
    bands, nodes, _ = adj_ref.shape
    reach = (bands - 1) // 2
    width = own_ref.shape[0]
    (own_copy,) = fetch([own_ref], near, here)
    copies = fetch([adj_ref.at[band] for band in range(bands)], buffer, arrived)
    ones = jnp.ones((16, nodes), BF16)
    degree = jnp.zeros((16, nodes), F32)
    for band in range(bands):
        copies[band].wait()
        for row in range(nodes // TILE):
            for column in range(nodes // TILE):
                keep = mask_ref[row, column, band].astype(F32).astype(BF16)
                rows, columns = pl.ds(row * TILE, TILE), pl.ds(column * TILE, TILE)
                weighted_ref[band, rows, columns] = buffer[band, rows, columns] * keep
        if band == reach:
            own_copy.wait()
            both = dot(jnp.concatenate([near[0], ones], axis=0), weighted_ref[band], LAST)
            base_ref[...] = both[:width]
            degree = degree + both[width:]
        else:
            degree = degree + dot(ones, weighted_ref[band], LAST)
    inverse_ref[...] = 1.0 / jnp.maximum(degree[:8], 1.0)


def mean_kernel(*refs):
    *near_refs, weighted_ref, base_ref, inverse_ref, out_ref, buffer, arrived = refs
    copies = fetch(near_refs, buffer, arrived)
    bands = weighted_ref.shape[0]
    reach = (bands - 1) // 2
    total = base_ref[...]
    for slot, band in enumerate([b for b in range(bands) if b != reach]):
        copies[slot].wait()
        total = total + dot(buffer[slot], weighted_ref[band], LAST)
    mean = (total * inverse_ref[0:1, :]).astype(BF16)
    for copy in range(out_ref.shape[0]):
        out_ref[copy] = mean


def act_kernel(scale, early_ref, means_ref, cot_ref, act_ref, grad_ref, partial_ref):
    groups, width, nodes = means_ref.shape
    total = groups * width
    feats = early_ref[:, :, :nodes].reshape(total, nodes)
    columns = early_ref[:, :, nodes:].reshape(total, 2 * width)
    means = means_ref[...].reshape(total, nodes)
    preact = dot(columns, feats, FIRST)[:width] + dot(columns, means, FIRST)[width:]
    sigmoid_z = 1.0 / (1.0 + jnp.exp(-preact))
    act_ref[...] = (preact * sigmoid_z).astype(BF16)
    slope = sigmoid_z * (1.0 + preact * (1.0 - sigmoid_z))
    grad = (cot_ref[...].astype(F32) * slope).astype(BF16)
    grad_ref[...] = grad
    stacked = jnp.concatenate(
        [feats.reshape(groups, width, nodes), means.reshape(groups, width, nodes)], axis=1
    ).reshape(2 * total, nodes)
    partial = dot(grad, stacked, LAST) * scale
    rows = width // partial_ref.shape[0]
    for piece in range(partial_ref.shape[0]):
        part = partial[piece * rows : (piece + 1) * rows]
        partial_ref[piece] = jnp.concatenate([part[:, :total], part[:, total:]], axis=0).astype(BF16)


def sum_y_kernel(in_ref, *refs):
    out_ref = refs[-1]
    total = in_ref[0].astype(F32)
    for part in range(1, in_ref.shape[0]):
        total = total + in_ref[part].astype(F32)
    total = total.astype(BF16)
    for copy in range(out_ref.shape[0]):
        out_ref[copy] = total


def sum_z_kernel(groups, lines, in_ref, *refs):
    out_ref = refs[-1]
    total = in_ref[0].astype(F32)
    for part in range(1, in_ref.shape[0]):
        total = total + in_ref[part].astype(F32)
    rows, lanes = out_ref.shape[1:]
    per_row = total.shape[1] // lanes
    for group in range(groups):
        up, across = group // per_row, group % per_row
        share = total[up * rows : (up + 1) * rows, across * lanes : (across + 1) * lanes]
        for line in range(lines):
            out_ref[group * lines + line] = share.astype(BF16)


def final_kernel(in_ref, self_ref, neigh_ref):
    sources, rows, lanes = in_ref.shape
    turned = in_ref[...].astype(F32).reshape(sources * rows, lanes).T
    half = lanes // 2
    self_ref[...] = turned[:half]
    neigh_ref[...] = turned[half:]


def back_kernel(place_ref, wself_ref, wneigh_ref, *refs):
    parts = place_ref.shape[0]
    grad_refs, (weighted_ref, inverse_ref), outs = refs[:parts], refs[parts : parts + 2], refs[parts + 2 : -2]
    buffer, arrived = refs[-2:]
    copies = fetch(grad_refs, buffer, arrived)
    bands = weighted_ref.shape[0]
    reach = (bands - 1) // 2
    depth = grad_refs[0].shape[0]
    for part, grad_ref in enumerate(grad_refs):
        lanes = pl.ds(pl.multiple_of(place_ref[part] * depth, depth), depth)
        copies[part].wait()
        neigh_part = dot(wneigh_ref[:, lanes], buffer[part], PLAIN)
        self_part = dot(wself_ref[:, lanes], buffer[part], PLAIN)
        neigh = neigh_part if part == 0 else neigh + neigh_part
        stays = self_part if part == 0 else stays + self_part
    spread = (neigh * inverse_ref[0:1, :]).astype(BF16)
    term_refs, base_ref = outs[:-1], outs[-1]
    others = [b for b in range(bands) if b != reach]
    for term_ref, band in zip(term_refs, others):
        term_ref[...] = dot(spread, weighted_ref[band], PLAIN).astype(BF16)
    base_ref[...] = stays + dot(spread, weighted_ref[reach], PLAIN)


def from_behind(value, steps):
    count = lax.axis_size(ROW)
    pairs = [(source, (source + steps) % count) for source in range(count)]
    return lax.ppermute(value, ROW, pairs)


def around(value, steps):
    count = lax.axis_size("x")
    pairs = [(source, (source + steps) % count) for source in range(count)]
    return lax.ppermute(value, "x", pairs)


def exchange(chunks, axes):
    return lax.all_to_all(chunks, axes, 0, 0, tiled=True)


def body(features, adjacency, tile_mask, w_self, w_neigh, cotangent):
    own = features.T
    width, nodes = own.shape
    groups = lax.axis_size(COL)
    lines = lax.axis_size("y")
    planes = lax.axis_size("z")
    total = groups * width
    bands = tile_mask.shape[1]
    reach = (bands - 1) // 2
    offsets = [k for k in range(-reach, reach + 1) if k != 0]
    shape = jax.ShapeDtypeStruct

    out_columns = local_call(
        prep_kernel,
        shape((groups, width, nodes + 2 * width), BF16),
        [ANY] * 3,
        (own, w_self, w_neigh),
        adjacency.size // 8,
        slots(3, (width, nodes)),
    )
    early = exchange(out_columns, COL)
    neighbours = [from_behind(own, -k) for k in offsets]

    panel = (width, nodes)
    adj = adjacency.transpose(1, 0, 2)
    weighted, base, inverse = local_call(
        mask_kernel,
        (shape(adj.shape, BF16), shape(panel, F32), shape((8, nodes), F32)),
        [SMEM, ANY, ANY, ANY],
        (tile_mask.transpose(0, 2, 1), own, adj, early),
        2 * adj.size,
        slots(bands, (nodes, nodes)) + slots(1, panel),
    )
    copies = local_call(
        mean_kernel,
        shape((groups, *panel), BF16),
        [ANY] * len(offsets) + [VMEM] * 3,
        (*neighbours, weighted, base, inverse),
        2 * adj.size,
        slots(len(offsets), panel),
    )
    means = exchange(copies, COL)

    grad_scale = 1.0 / math.sqrt(lax.axis_size(ROW) * nodes)

    def act(*refs):
        act_kernel(grad_scale, *refs)

    activated, grad_preact, partial = local_call(
        act,
        (shape(panel, BF16), shape(panel, BF16), shape((lines, 2 * (width // lines), total), BF16)),
        [VMEM] * 3,
        (early, means, cotangent.T),
        2 * adj.size,
    )

    over_y = exchange(partial, "y")

    pair = lax.all_gather(grad_preact, "core", axis=0, tiled=True)
    sides = [pair] + [around(pair, k) for k in range(1, lax.axis_size("x"))]

    folded = local_call(
        sum_y_kernel,
        shape((planes, 2 * (width // lines), total), BF16),
        [VMEM] + [ANY] * len(sides),
        (over_y, *sides),
        adj.size,
    )
    over_z = exchange(folded, "z")

    places = lax.rem(
        lax.axis_index("x") - jnp.arange(len(sides), dtype=jnp.int32) + len(sides), len(sides)
    ).astype(jnp.int32)
    *terms, stays = local_call(
        back_kernel,
        (*[shape(panel, BF16)] * len(offsets), shape(panel, F32)),
        [SMEM, VMEM, VMEM] + [ANY] * len(sides) + [VMEM] * 2,
        (places, w_self, w_neigh, *sides, weighted, inverse),
        2 * adj.size,
        slots(len(sides), pair.shape),
    )
    arrived = [from_behind(term, k) for term, k in zip(terms, offsets)]

    def sum_z(*refs):
        sum_z_kernel(groups, lines, *refs)

    shares = local_call(
        sum_z,
        shape((groups * lines, width // lines, 2 * width), BF16),
        [VMEM] + [ANY] * len(arrived),
        (over_z, *arrived),
        adj.size,
    )
    gathered = exchange(shares, COL + ("y",))
    grad_self, grad_neigh = local_call(
        final_kernel,
        (shape((width, total), F32), shape((width, total), F32)),
        [VMEM],
        (gathered,),
        adj.size,
    )
    for term in arrived:
        stays = stays + term.astype(F32)
    return (activated.T, stays.astype(BF16).T, grad_self, grad_neigh)


def solution(mesh):
    rows, columns = mesh.devices.shape
    lines = math.gcd(rows, 8)
    cores = math.gcd(columns, 2)
    fine = Mesh(
        mesh.devices.reshape(rows // lines, lines, columns // cores, cores), ROW + COL
    )
    return jax.shard_map(
        body,
        mesh=fine,
        in_specs=(
            P(ROW, COL),
            P(ROW, None, None),
            P(ROW, None, None),
            P(COL, None),
            P(COL, None),
            P(ROW, COL),
        ),
        out_specs=(P(ROW, COL), P(ROW, COL), P(COL, None), P(COL, None)),
        check_vma=False,
    )
```

```python
import math

import jax
import jax.numpy as jnp
from jax import lax
from jax.experimental import pallas as pl
from jax.experimental.pallas import tpu as pltpu
from jax.sharding import Mesh
from jax.sharding import PartitionSpec as P

ROW = ("z", "y")
COL = ("x", "core")
TILE = 128
SPLIT = 1
LAST = (((1,), (1,)), ((), ()))
FIRST = (((0,), (0,)), ((), ()))
PLAIN = (((1,), (0,)), ((), ()))
VMEM = pl.BlockSpec(memory_space=pltpu.VMEM)
SMEM = pl.BlockSpec(memory_space=pltpu.SMEM)
ANY = pl.BlockSpec(memory_space=pl.ANY)
BF16 = jnp.bfloat16
F32 = jnp.float32


def local_call(kernel, out_shape, in_specs, args, flops):
    outs = jax.tree.leaves(out_shape)
    moved = sum(a.size * a.dtype.itemsize for a in (*args, *outs))
    return pl.pallas_call(
        kernel,
        out_shape=out_shape,
        in_specs=in_specs,
        out_specs=jax.tree.map(lambda _: VMEM, out_shape),
        compiler_params=pltpu.CompilerParams(vmem_limit_bytes=24 * 1024 * 1024),
        cost_estimate=pl.CostEstimate(flops=flops, bytes_accessed=moved, transcendentals=0),
    )(*args)


def dot(a, b, dims):
    return lax.dot_general(a, b, dims, preferred_element_type=F32)


def mask_kernel(mask_ref, own_ref, adj_ref, weighted_ref, base_ref, inverse_ref):
    bands, nodes, _ = adj_ref.shape
    reach = (bands - 1) // 2
    width = own_ref.shape[0]
    ones = jnp.ones((16, nodes), BF16)
    degree = jnp.zeros((16, nodes), F32)
    for band in range(bands):
        for row in range(nodes // TILE):
            for column in range(nodes // TILE):
                keep = mask_ref[row, column, band].astype(F32).astype(BF16)
                rows, columns = pl.ds(row * TILE, TILE), pl.ds(column * TILE, TILE)
                weighted_ref[band, rows, columns] = adj_ref[band, rows, columns] * keep
        if band == reach:
            both = dot(jnp.concatenate([own_ref[...], ones], axis=0), weighted_ref[band], LAST)
            base_ref[...] = both[:width]
            degree = degree + both[width:]
        else:
            degree = degree + dot(ones, weighted_ref[band], LAST)
    inverse_ref[...] = 1.0 / jnp.maximum(degree[:8], 1.0)


def mean_kernel(*refs):
    *near_refs, weighted_ref, base_ref, inverse_ref, own_ref, wself_ref, wneigh_ref = refs[:-2]
    mean_ref, partial_ref = refs[-2:]
    bands = weighted_ref.shape[0]
    reach = (bands - 1) // 2
    total = base_ref[...]
    for near_ref, band in zip(near_refs, [b for b in range(bands) if b != reach]):
        total = total + dot(near_ref[...], weighted_ref[band], LAST)
    mean = (total * inverse_ref[0:1, :]).astype(BF16)
    mean_ref[...] = mean
    weights = jnp.concatenate([wself_ref[...], wneigh_ref[...]], axis=0)
    values = jnp.concatenate([own_ref[...], mean], axis=0)
    partial_ref[...] = dot(weights, values, FIRST).astype(BF16).reshape(partial_ref.shape)


def act_kernel(parts_ref, cot_ref, act_ref, grad_ref):
    preact = parts_ref[0].astype(F32)
    for part in range(1, parts_ref.shape[0]):
        preact = preact + parts_ref[part].astype(F32)
    sigmoid_z = 1.0 / (1.0 + jnp.exp(-preact))
    act_ref[...] = (preact * sigmoid_z).astype(BF16)
    slope = sigmoid_z * (1.0 + preact * (1.0 - sigmoid_z))
    grad = (cot_ref[...].astype(F32) * slope).astype(BF16)
    for copy in range(grad_ref.shape[0]):
        grad_ref[copy] = grad


def weight_kernel(scale, grads_ref, own_ref, mean_ref, pieces_ref):
    groups, width, nodes = grads_ref.shape
    values = jnp.concatenate([own_ref[...], mean_ref[...]], axis=0)
    term = dot(values, grads_ref[...].reshape(groups * width, nodes), LAST) * scale
    pieces_ref[...] = term.astype(BF16).reshape(pieces_ref.shape)


def sum_kernel(in_ref, *refs):
    out_ref = refs[-1]
    total = in_ref[0].astype(F32)
    for part in range(1, in_ref.shape[0]):
        total = total + in_ref[part].astype(F32)
    total = total.astype(BF16)
    for copy in range(out_ref.shape[0]):
        out_ref[copy] = total


def final_kernel(in_ref, self_ref, neigh_ref):
    total = in_ref[...].astype(F32).reshape(in_ref.shape[0] * in_ref.shape[1], in_ref.shape[2])
    half = self_ref.shape[0]
    self_ref[...] = total[:half]
    neigh_ref[...] = total[half:]


def back_kernel(grads_ref, wself_ref, wneigh_ref, weighted_ref, inverse_ref, *outs):
    groups, width, nodes = grads_ref.shape
    bands = weighted_ref.shape[0]
    reach = (bands - 1) // 2
    grads = grads_ref[...].reshape(groups * width, nodes)
    spread = (dot(wneigh_ref[...], grads, PLAIN) * inverse_ref[0:1, :]).astype(BF16)
    term_refs, stays_ref = outs[:-1], outs[-1]
    for term_ref, band in zip(term_refs, [b for b in range(bands) if b != reach]):
        term_ref[...] = dot(spread, weighted_ref[band], PLAIN).astype(BF16)
    stays_ref[...] = dot(wself_ref[...], grads, PLAIN) + dot(spread, weighted_ref[reach], PLAIN)


def from_behind(value, steps):
    count = lax.axis_size(ROW)
    pairs = [(source, (source + steps) % count) for source in range(count)]
    return lax.ppermute(value, ROW, pairs)


def exchange(chunks, axes):
    return lax.all_to_all(chunks, axes, 0, 0, tiled=True)


def body(features, adjacency, tile_mask, w_self, w_neigh, cotangent):
    own = features.T
    panel = width, nodes = own.shape
    groups = lax.axis_size(COL)
    lines = lax.axis_size("y")
    planes = lax.axis_size("z")
    total = groups * width
    bands = tile_mask.shape[1]
    reach = (bands - 1) // 2
    offsets = [k for k in range(-reach, reach + 1) if k != 0]
    shape = jax.ShapeDtypeStruct
    everyone = shape((groups, *panel), BF16)

    neighbours = [from_behind(own, -k) for k in offsets]
    adj = adjacency.transpose(1, 0, 2)
    weighted, base, inverse = local_call(
        mask_kernel,
        (shape(adj.shape, BF16), shape(panel, F32), shape((8, nodes), F32)),
        [SMEM, VMEM, VMEM],
        (tile_mask.transpose(0, 2, 1), own, adj),
        2 * adj.size,
    )
    mean, shares = local_call(
        mean_kernel,
        (shape(panel, BF16), everyone),
        [VMEM] * (len(offsets) + 6),
        (*neighbours, weighted, base, inverse, own, w_self, w_neigh),
        2 * adj.size,
    )
    activated, copies = local_call(
        act_kernel,
        (shape(panel, BF16), everyone),
        [VMEM] * 2,
        (exchange(shares, COL), cotangent.T),
        adj.size,
    )
    grads = exchange(copies, COL)

    grad_scale = 1.0 / math.sqrt(lax.axis_size(ROW) * nodes)

    def weight_terms(*refs):
        weight_kernel(grad_scale, *refs)

    height = 2 * width // lines
    pieces = local_call(
        weight_terms,
        shape((lines, height, total), BF16),
        [VMEM] * 3,
        (grads, own, mean),
        adj.size,
    )
    over_y = exchange(pieces, "y")

    *terms, stays = local_call(
        back_kernel,
        (*[shape(panel, BF16)] * len(offsets), shape(panel, F32)),
        [VMEM] * 5,
        (grads, w_self, w_neigh, weighted, inverse),
        2 * adj.size,
    )
    arrived = [from_behind(term, k) for term, k in zip(terms, offsets)]
    early, late = arrived[:SPLIT], arrived[SPLIT:]

    folded = local_call(
        sum_kernel,
        shape((planes, height, total), BF16),
        [VMEM] + [ANY] * len(early),
        (over_y, *early),
        adj.size,
    )
    over_z = exchange(folded, "z")
    summed = local_call(
        sum_kernel,
        shape((lines, height, total), BF16),
        [VMEM] + [ANY] * len(late),
        (over_z, *late),
        adj.size,
    )
    gathered = exchange(summed, "y")
    grad_self, grad_neigh = local_call(
        final_kernel,
        (shape((width, total), F32), shape((width, total), F32)),
        [VMEM],
        (gathered,),
        adj.size,
    )
    for term in arrived:
        stays = stays + term.astype(F32)
    return (activated.T, stays.astype(BF16).T, grad_self, grad_neigh)


def solution(mesh):
    rows, columns = mesh.devices.shape
    lines = math.gcd(rows, 8)
    cores = math.gcd(columns, 2)
    fine = Mesh(
        mesh.devices.reshape(rows // lines, lines, columns // cores, cores), ROW + COL
    )
    return jax.shard_map(
        body,
        mesh=fine,
        in_specs=(
            P(ROW, COL),
            P(ROW, None, None),
            P(ROW, None, None),
            P(COL, None),
            P(COL, None),
            P(ROW, COL),
        ),
        out_specs=(P(ROW, COL), P(ROW, COL), P(COL, None), P(COL, None)),
        check_vma=False,
    )
```

```python
import math

import jax
import jax.numpy as jnp
from jax import lax
from jax.experimental import pallas as pl
from jax.experimental.pallas import tpu as pltpu
from jax.sharding import Mesh
from jax.sharding import PartitionSpec as P

ROW = ("z", "y")
COL = ("x", "core")
TILE = 128
LAST = (((1,), (1,)), ((), ()))
FIRST = (((0,), (0,)), ((), ()))
PLAIN = (((1,), (0,)), ((), ()))
VMEM = pl.BlockSpec(memory_space=pltpu.VMEM)
SMEM = pl.BlockSpec(memory_space=pltpu.SMEM)
ANY = pl.BlockSpec(memory_space=pl.ANY)
BF16 = jnp.bfloat16
F32 = jnp.float32


def local_call(kernel, out_shape, in_specs, args, flops, scratch=()):
    outs = jax.tree.leaves(out_shape)
    moved = sum(a.size * a.dtype.itemsize for a in (*args, *outs))
    return pl.pallas_call(
        kernel,
        out_shape=out_shape,
        in_specs=in_specs,
        out_specs=jax.tree.map(lambda _: VMEM, out_shape),
        scratch_shapes=[pltpu.VMEM(size, F32) for size in scratch],
        compiler_params=pltpu.CompilerParams(vmem_limit_bytes=24 * 1024 * 1024),
        cost_estimate=pl.CostEstimate(flops=flops, bytes_accessed=moved, transcendentals=0),
    )(*args)


def dot(a, b, dims):
    return lax.dot_general(a, b, dims, preferred_element_type=F32)


def mask_kernel(mask_ref, pair_ref, adj_ref, weighted_ref, base_ref, inverse_ref):
    bands, nodes, _ = adj_ref.shape
    reach = (bands - 1) // 2
    depth = base_ref.shape[0]
    ones = jnp.ones((16, nodes), BF16)
    degree = jnp.zeros((16, nodes), F32)
    for band in range(bands):
        for row in range(nodes // TILE):
            for column in range(nodes // TILE):
                keep = mask_ref[row, column, band].astype(F32).astype(BF16)
                rows, columns = pl.ds(row * TILE, TILE), pl.ds(column * TILE, TILE)
                weighted_ref[band, rows, columns] = adj_ref[band, rows, columns] * keep
        if band == reach:
            pair = pair_ref[...].reshape(depth, nodes)
            both = dot(jnp.concatenate([pair, ones], axis=0), weighted_ref[band], LAST)
            base_ref[...] = both[:depth]
            degree = degree + both[depth:]
        else:
            degree = degree + dot(ones, weighted_ref[band], LAST)
    inverse_ref[...] = 1.0 / jnp.maximum(degree[:8], 1.0)


def near_kernel(core_ref, behind_ref, ahead_ref, weighted_ref, out_ref):
    reach = (weighted_ref.shape[0] - 1) // 2
    steps = core_ref[0] + 1
    total = dot(behind_ref[...], weighted_ref[reach - steps], LAST)
    out_ref[...] = total + dot(ahead_ref[...], weighted_ref[reach + steps], LAST)


def mean_kernel(
    core_ref, near_ref, base_ref, inverse_ref, pair_ref, wself_ref, wneigh_ref, mean_ref, out_ref, scratch
):
    cores, width, nodes = pair_ref.shape
    depth = cores * width
    core = core_ref[0]
    total = base_ref[...]
    for part in range(cores):
        total = total + near_ref[part]
    mean = (total * inverse_ref[0:1, :]).astype(BF16)
    scratch[:depth] = total * inverse_ref[0:1, :]
    mean_ref[...] = scratch[pl.ds(pl.multiple_of(core * width, width), width), :].astype(BF16)
    weights = jnp.concatenate(
        [w[...].reshape(depth, w.shape[2]) for w in (wself_ref, wneigh_ref)], axis=0
    )
    values = jnp.concatenate([pair_ref[...].reshape(depth, nodes), mean], axis=0)
    scratch[...] = dot(weights, values, FIRST)
    for chip in range(out_ref.shape[0]):
        first = pl.multiple_of((chip * cores + core) * width, width)
        out_ref[chip] = scratch[pl.ds(first, width), :].astype(BF16)


def act_kernel(parts_ref, cot_ref, act_ref, grad_ref):
    preact = parts_ref[0].astype(F32)
    for part in range(1, parts_ref.shape[0]):
        preact = preact + parts_ref[part].astype(F32)
    sigmoid_z = 1.0 / (1.0 + jnp.exp(-preact))
    act_ref[...] = (preact * sigmoid_z).astype(BF16)
    slope = sigmoid_z * (1.0 + preact * (1.0 - sigmoid_z))
    grad = (cot_ref[...].astype(F32) * slope).astype(BF16)
    for copy in range(grad_ref.shape[0]):
        grad_ref[copy] = grad


def weight_kernel(scale, grads_ref, own_ref, mean_ref, pieces_ref):
    groups, width, nodes = grads_ref.shape
    values = jnp.concatenate([own_ref[...], mean_ref[...]], axis=0)
    term = dot(values, grads_ref[...].reshape(groups * width, nodes), LAST) * scale
    pieces_ref[...] = term.astype(BF16).reshape(pieces_ref.shape)


def sum_kernel(in_ref, *refs):
    out_ref = refs[-1]
    total = in_ref[0].astype(F32)
    for part in range(1, in_ref.shape[0]):
        total = total + in_ref[part].astype(F32)
    total = total.astype(BF16)
    for copy in range(out_ref.shape[0]):
        out_ref[copy] = total


def final_kernel(in_ref, self_ref, neigh_ref):
    total = in_ref[...].astype(F32).reshape(in_ref.shape[0] * in_ref.shape[1], in_ref.shape[2])
    half = self_ref.shape[0]
    self_ref[...] = total[:half]
    neigh_ref[...] = total[half:]


def back_kernel(
    core_ref, grads_ref, wself_ref, wneigh_ref, weighted_ref, inverse_ref, behind_ref, ahead_ref, stays_ref, scratch
):
    groups, width, nodes = grads_ref.shape
    reach = (weighted_ref.shape[0] - 1) // 2
    depth = scratch.shape[0]
    core = core_ref[0]
    steps = core + 1
    grads = grads_ref[...].reshape(groups * width, nodes)
    wneigh = wneigh_ref[...].reshape(depth, groups * width)
    spread = (dot(wneigh, grads, PLAIN) * inverse_ref[0:1, :]).astype(BF16)
    behind_ref[...] = dot(spread, weighted_ref[reach - steps], PLAIN).astype(BF16)
    ahead_ref[...] = dot(spread, weighted_ref[reach + steps], PLAIN).astype(BF16)
    scratch[...] = dot(spread, weighted_ref[reach], PLAIN)
    own = scratch[pl.ds(pl.multiple_of(core * width, width), width), :]
    stays_ref[...] = dot(wself_ref[...], grads, PLAIN) + own


def out_kernel(core_ref, stays_ref, *refs):
    *term_refs, out_ref = refs
    width = out_ref.shape[0]
    total = stays_ref[...]
    rows = pl.ds(pl.multiple_of(core_ref[0] * width, width), width)
    for term_ref in term_refs:
        for part in range(term_ref.shape[0]):
            total = total + term_ref[part, rows, :].astype(F32)
    out_ref[...] = total.astype(BF16)


def shift(value, sign):
    axes = ROW + ("core",)
    cores = lax.axis_size("core")
    count = lax.axis_size(ROW)
    pairs = [
        (source * cores + core, (source + sign * (core + 1)) % count * cores + core)
        for source in range(count)
        for core in range(cores)
    ]
    return lax.ppermute(value, axes, pairs)


def of_chip(value):
    return lax.all_gather(value, "core", axis=0, tiled=False)


def exchange(chunks, axes):
    return lax.all_to_all(chunks, axes, 0, 0, tiled=True)


def body(features, adjacency, tile_mask, w_self, w_neigh, cotangent):
    own = features.T
    panel = width, nodes = own.shape
    groups = lax.axis_size(COL)
    lines = lax.axis_size("y")
    planes = lax.axis_size("z")
    total = groups * width
    cores = lax.axis_size("core")
    chips = lax.axis_size("x")
    depth = cores * width
    shape = jax.ShapeDtypeStruct
    wide = (depth, nodes)
    core = lax.axis_index("core").astype(jnp.int32).reshape(1)

    pair = of_chip(own)
    behind = shift(pair.reshape(wide), 1)
    ahead = shift(pair.reshape(wide), -1)
    wself_pair, wneigh_pair = of_chip(w_self), of_chip(w_neigh)
    adj = adjacency.transpose(1, 0, 2)
    weighted, base, inverse = local_call(
        mask_kernel,
        (shape(adj.shape, BF16), shape(wide, F32), shape((8, nodes), F32)),
        [SMEM, VMEM, VMEM],
        (tile_mask.transpose(0, 2, 1), pair, adj),
        2 * adj.size,
    )
    near = local_call(
        near_kernel,
        shape(wide, F32),
        [SMEM] + [VMEM] * 3,
        (core, behind, ahead, weighted),
        2 * adj.size,
    )
    mean, shares = local_call(
        mean_kernel,
        (shape(panel, BF16), shape((chips, *panel), BF16)),
        [SMEM] + [VMEM] * 6,
        (core, of_chip(near), base, inverse, pair, wself_pair, wneigh_pair),
        2 * adj.size,
        [(total, nodes)],
    )
    activated, copies = local_call(
        act_kernel,
        (shape(panel, BF16), shape((groups, *panel), BF16)),
        [VMEM] * 2,
        (exchange(shares, "x"), cotangent.T),
        adj.size,
    )
    grads = exchange(copies, COL)

    grad_scale = 1.0 / math.sqrt(lax.axis_size(ROW) * nodes)

    def weight_terms(*refs):
        weight_kernel(grad_scale, *refs)

    height = 2 * width // lines
    pieces = local_call(
        weight_terms,
        shape((lines, height, total), BF16),
        [VMEM] * 3,
        (grads, own, mean),
        adj.size,
    )
    over_y = exchange(pieces, "y")

    to_behind, to_ahead, stays = local_call(
        back_kernel,
        (shape(wide, BF16), shape(wide, BF16), shape(panel, F32)),
        [SMEM] + [VMEM] * 5,
        (core, grads, w_self, wneigh_pair, weighted, inverse),
        2 * adj.size,
        [wide],
    )
    arrived = [shift(to_behind, -1), shift(to_ahead, 1)]

    folded = local_call(
        sum_kernel,
        shape((planes, height, total), BF16),
        [VMEM],
        (over_y,),
        adj.size,
    )
    over_z = exchange(folded, "z")
    summed = local_call(
        sum_kernel,
        shape((lines, height, total), BF16),
        [VMEM] + [ANY] * len(arrived),
        (over_z, *arrived),
        adj.size,
    )
    gathered = exchange(summed, "y")
    grad_self, grad_neigh = local_call(
        final_kernel,
        (shape((width, total), F32), shape((width, total), F32)),
        [VMEM],
        (gathered,),
        adj.size,
    )
    grad_features = local_call(
        out_kernel,
        shape(panel, BF16),
        [SMEM] + [VMEM] * (1 + len(arrived)),
        (core, stays, *[of_chip(term) for term in arrived]),
        adj.size,
    )
    return (activated.T, grad_features.T, grad_self, grad_neigh)


def solution(mesh):
    rows, columns = mesh.devices.shape
    lines = math.gcd(rows, 8)
    cores = math.gcd(columns, 2)
    fine = Mesh(
        mesh.devices.reshape(rows // lines, lines, columns // cores, cores), ROW + COL
    )
    return jax.shard_map(
        body,
        mesh=fine,
        in_specs=(
            P(ROW, COL),
            P(ROW, None, None),
            P(ROW, None, None),
            P(COL, None),
            P(COL, None),
            P(ROW, COL),
        ),
        out_specs=(P(ROW, COL), P(ROW, COL), P(COL, None), P(COL, None)),
        check_vma=False,
    )
```

```python
import math

import jax
import jax.numpy as jnp
from jax import lax
from jax.experimental import pallas as pl
from jax.experimental.pallas import tpu as pltpu
from jax.sharding import Mesh
from jax.sharding import PartitionSpec as P

ROW = ("z", "y")
COL = ("x", "core")
TILE = 128
LAST = (((1,), (1,)), ((), ()))
FIRST = (((0,), (0,)), ((), ()))
PLAIN = (((1,), (0,)), ((), ()))
VMEM = pl.BlockSpec(memory_space=pltpu.VMEM)
SMEM = pl.BlockSpec(memory_space=pltpu.SMEM)
ANY = pl.BlockSpec(memory_space=pl.ANY)
BF16 = jnp.bfloat16
F32 = jnp.float32


def local_call(kernel, out_shape, in_specs, args, flops, scratch=()):
    outs = jax.tree.leaves(out_shape)
    moved = sum(a.size * a.dtype.itemsize for a in (*args, *outs))
    return pl.pallas_call(
        kernel,
        out_shape=out_shape,
        in_specs=in_specs,
        out_specs=jax.tree.map(lambda _: VMEM, out_shape),
        scratch_shapes=[pltpu.VMEM(size, F32) for size in scratch],
        compiler_params=pltpu.CompilerParams(vmem_limit_bytes=24 * 1024 * 1024),
        cost_estimate=pl.CostEstimate(flops=flops, bytes_accessed=moved, transcendentals=0),
    )(*args)


def dot(a, b, dims):
    return lax.dot_general(a, b, dims, preferred_element_type=F32)


def mask_kernel(mask_ref, pair_ref, adj_ref, *refs):
    weighted_ref, base_ref, inverse_ref = refs[-3:]
    bands, nodes, _ = adj_ref.shape
    reach = (bands - 1) // 2
    depth = base_ref.shape[0]
    ones = jnp.ones((16, nodes), BF16)
    degree = jnp.zeros((16, nodes), F32)
    for band in range(bands):
        for row in range(nodes // TILE):
            for column in range(nodes // TILE):
                keep = mask_ref[row, column, band].astype(F32).astype(BF16)
                rows, columns = pl.ds(row * TILE, TILE), pl.ds(column * TILE, TILE)
                weighted_ref[band, rows, columns] = adj_ref[band, rows, columns] * keep
        if band == reach:
            pair = pair_ref[...].reshape(depth, nodes)
            both = dot(jnp.concatenate([pair, ones], axis=0), weighted_ref[band], LAST)
            base_ref[...] = both[:depth]
            degree = degree + both[depth:]
        else:
            degree = degree + dot(ones, weighted_ref[band], LAST)
    inverse_ref[...] = 1.0 / jnp.maximum(degree[:8], 1.0)


def near_kernel(core_ref, behind_ref, ahead_ref, weighted_ref, out_ref):
    reach = (weighted_ref.shape[0] - 1) // 2
    steps = core_ref[0] + 1
    total = dot(behind_ref[...], weighted_ref[reach - steps], LAST)
    out_ref[...] = total + dot(ahead_ref[...], weighted_ref[reach + steps], LAST)


def mean_kernel(
    core_ref, near_ref, base_ref, inverse_ref, pair_ref, wself_ref, wneigh_ref, mean_ref, out_ref, scratch
):
    cores, width, nodes = pair_ref.shape
    depth = cores * width
    core = core_ref[0]
    total = base_ref[...]
    for part in range(cores):
        total = total + near_ref[part]
    mean = (total * inverse_ref[0:1, :]).astype(BF16)
    mean_ref[...] = mean
    weights = jnp.concatenate(
        [w[...].reshape(depth, w.shape[2]) for w in (wself_ref, wneigh_ref)], axis=0
    )
    values = jnp.concatenate([pair_ref[...].reshape(depth, nodes), mean], axis=0)
    scratch[...] = dot(weights, values, FIRST)
    for chip in range(out_ref.shape[0]):
        first = pl.multiple_of((chip * cores + core) * width, width)
        out_ref[chip] = scratch[pl.ds(first, width), :].astype(BF16)


def act_kernel(parts_ref, cot_ref, act_ref, grad_ref):
    preact = parts_ref[0].astype(F32)
    for part in range(1, parts_ref.shape[0]):
        preact = preact + parts_ref[part].astype(F32)
    sigmoid_z = 1.0 / (1.0 + jnp.exp(-preact))
    act_ref[...] = (preact * sigmoid_z).astype(BF16)
    slope = sigmoid_z * (1.0 + preact * (1.0 - sigmoid_z))
    grad = (cot_ref[...].astype(F32) * slope).astype(BF16)
    for copy in range(grad_ref.shape[0]):
        grad_ref[copy] = grad


def weight_kernel(scale, grads_ref, pair_ref, mean_ref, pieces_ref):
    chips, width, nodes = grads_ref.shape
    lines, cores, height, columns = pieces_ref.shape
    values = [
        ref[core * width : (core + 1) * width]
        for core in range(cores)
        for ref in (pair_ref[...].reshape(cores * width, nodes), mean_ref[...])
    ]
    grads = grads_ref[...].reshape(columns, nodes)
    term = dot(jnp.concatenate(values, axis=0), grads, LAST) * scale
    for line in range(lines):
        for core in range(cores):
            first = core * lines * height + line * height
            pieces_ref[line, core] = term[first : first + height].astype(BF16)


def sum_kernel(in_ref, *refs):
    out_ref = refs[-1]
    total = in_ref[0].astype(F32)
    for part in range(1, in_ref.shape[0]):
        total = total + in_ref[part].astype(F32)
    total = total.astype(BF16).reshape(out_ref.shape[1:])
    for copy in range(out_ref.shape[0]):
        out_ref[copy] = total


def final_kernel(width, in_ref, self_ref, neigh_ref):
    lines, cores, height, columns = in_ref.shape
    parts = [in_ref[:, core].reshape(lines * height, columns).astype(F32) for core in range(cores)]
    half = self_ref.shape[0]
    for chip in range(columns // width):
        both = jnp.concatenate(
            [part[:, chip * width : (chip + 1) * width] for part in parts], axis=1
        )
        lanes = slice(chip * cores * width, (chip + 1) * cores * width)
        self_ref[:, lanes] = both[:half]
        neigh_ref[:, lanes] = both[half:]


def back_kernel(
    core_ref, grads_ref, wself_ref, wneigh_ref, weighted_ref, inverse_ref, behind_ref, ahead_ref, stays_ref, scratch
):
    cores, chips, width, nodes = grads_ref.shape
    groups = cores * chips
    reach = (weighted_ref.shape[0] - 1) // 2
    depth = scratch.shape[0]
    core = core_ref[0]
    steps = core + 1
    grads = jnp.concatenate(
        [grads_ref[part, chip] for chip in range(chips) for part in range(cores)], axis=0
    )
    wneigh = wneigh_ref[...].reshape(depth, groups * width)
    spread = (dot(wneigh, grads, PLAIN) * inverse_ref[0:1, :]).astype(BF16)
    behind_ref[...] = dot(spread, weighted_ref[reach - steps], PLAIN).astype(BF16)
    ahead_ref[...] = dot(spread, weighted_ref[reach + steps], PLAIN).astype(BF16)
    scratch[...] = dot(spread, weighted_ref[reach], PLAIN)
    own = scratch[pl.ds(pl.multiple_of(core * width, width), width), :]
    stays_ref[...] = dot(wself_ref[...], grads, PLAIN) + own


def out_kernel(core_ref, stays_ref, *refs):
    *term_refs, out_ref = refs
    width = out_ref.shape[0]
    total = stays_ref[...]
    rows = pl.ds(pl.multiple_of(core_ref[0] * width, width), width)
    for term_ref in term_refs:
        for part in range(term_ref.shape[0]):
            total = total + term_ref[part, rows, :].astype(F32)
    out_ref[...] = total.astype(BF16)


def shift(value, sign):
    axes = ROW + ("core",)
    cores = lax.axis_size("core")
    count = lax.axis_size(ROW)
    pairs = [
        (source * cores + core, (source + sign * (core + 1)) % count * cores + core)
        for source in range(count)
        for core in range(cores)
    ]
    return lax.ppermute(value, axes, pairs)


def of_chip(value):
    return lax.all_gather(value, "core", axis=0, tiled=False)


def exchange(chunks, axes):
    return lax.all_to_all(chunks, axes, 0, 0, tiled=True)


def body(features, adjacency, tile_mask, w_self, w_neigh, cotangent):
    own = features.T
    panel = width, nodes = own.shape
    groups = lax.axis_size(COL)
    lines = lax.axis_size("y")
    planes = lax.axis_size("z")
    total = groups * width
    cores = lax.axis_size("core")
    chips = lax.axis_size("x")
    depth = cores * width
    shape = jax.ShapeDtypeStruct
    wide = (depth, nodes)
    core = lax.axis_index("core").astype(jnp.int32).reshape(1)

    pair = of_chip(own)
    behind = shift(pair.reshape(wide), 1)
    ahead = shift(pair.reshape(wide), -1)
    wself_pair, wneigh_pair = of_chip(w_self), of_chip(w_neigh)
    adj = adjacency.transpose(1, 0, 2)
    weighted, base, inverse = local_call(
        mask_kernel,
        (shape(adj.shape, BF16), shape(wide, F32), shape((8, nodes), F32)),
        [SMEM, VMEM, VMEM, ANY, ANY],
        (tile_mask.transpose(0, 2, 1), pair, adj, wself_pair, wneigh_pair),
        2 * adj.size,
    )
    near = local_call(
        near_kernel,
        shape(wide, F32),
        [SMEM] + [VMEM] * 3,
        (core, behind, ahead, weighted),
        2 * adj.size,
    )
    mean, shares = local_call(
        mean_kernel,
        (shape(wide, BF16), shape((chips, *panel), BF16)),
        [SMEM] + [VMEM] * 6,
        (core, of_chip(near), base, inverse, pair, wself_pair, wneigh_pair),
        2 * adj.size,
        [(total, nodes)],
    )
    activated, copies = local_call(
        act_kernel,
        (shape(panel, BF16), shape((chips, *panel), BF16)),
        [VMEM] * 2,
        (exchange(shares, "x"), cotangent.T),
        adj.size,
    )
    grads = exchange(copies, "x")

    grad_scale = 1.0 / math.sqrt(lax.axis_size(ROW) * nodes)

    def weight_terms(*refs):
        weight_kernel(grad_scale, *refs)

    height = 2 * width // lines
    piece = (cores, height, chips * width)
    pieces = local_call(
        weight_terms,
        shape((lines, *piece), BF16),
        [VMEM] * 3,
        (grads, pair, mean),
        adj.size,
    )
    over_y = exchange(pieces, "y")

    to_behind, to_ahead, stays = local_call(
        back_kernel,
        (shape(wide, BF16), shape(wide, BF16), shape(panel, F32)),
        [SMEM] + [VMEM] * 5,
        (core, of_chip(grads), w_self, wneigh_pair, weighted, inverse),
        2 * adj.size,
        [wide],
    )
    arrived = [shift(to_behind, -1), shift(to_ahead, 1)]

    folded = local_call(
        sum_kernel,
        shape((planes, *piece), BF16),
        [VMEM, ANY],
        (over_y, stays),
        adj.size,
    )
    over_z = exchange(folded, "z")
    first, second = of_chip(arrived[0]), arrived[1]
    summed = local_call(
        sum_kernel,
        shape((lines, *piece), BF16),
        [VMEM, ANY, ANY],
        (over_z, first, second),
        adj.size,
    )
    gathered = exchange(summed.reshape(lines * cores, *piece[1:]), ("y", "core"))

    def final(*refs):
        final_kernel(width, *refs)

    grad_self, grad_neigh = local_call(
        final,
        (shape((width, total), F32), shape((width, total), F32)),
        [VMEM],
        (gathered.reshape(lines, *piece),),
        adj.size,
    )
    grad_features = local_call(
        out_kernel,
        shape(panel, BF16),
        [SMEM] + [VMEM] * (1 + len(arrived)),
        (core, stays, first, of_chip(second)),
        adj.size,
    )
    return (activated.T, grad_features.T, grad_self, grad_neigh)


def solution(mesh):
    rows, columns = mesh.devices.shape
    lines = math.gcd(rows, 8)
    cores = math.gcd(columns, 2)
    fine = Mesh(
        mesh.devices.reshape(rows // lines, lines, columns // cores, cores), ROW + COL
    )
    return jax.shard_map(
        body,
        mesh=fine,
        in_specs=(
            P(ROW, COL),
            P(ROW, None, None),
            P(ROW, None, None),
            P(COL, None),
            P(COL, None),
            P(ROW, COL),
        ),
        out_specs=(P(ROW, COL), P(ROW, COL), P(COL, None), P(COL, None)),
        check_vma=False,
    )
```

```python
import math

import jax
import jax.numpy as jnp
from jax import lax
from jax.experimental import pallas as pl
from jax.experimental.pallas import tpu as pltpu
from jax.sharding import Mesh
from jax.sharding import PartitionSpec as P

ROW = ("far", "near", "y")
BLOCK = ("near", "y")
COL = ("x", "core")
TILE = 128
LAST = (((1,), (1,)), ((), ()))
FIRST = (((0,), (0,)), ((), ()))
PLAIN = (((1,), (0,)), ((), ()))
VMEM = pl.BlockSpec(memory_space=pltpu.VMEM)
SMEM = pl.BlockSpec(memory_space=pltpu.SMEM)
ANY = pl.BlockSpec(memory_space=pl.ANY)
BF16 = jnp.bfloat16
F32 = jnp.float32


def local_call(kernel, out_shape, in_specs, args, flops, scratch=()):
    outs = jax.tree.leaves(out_shape)
    moved = sum(a.size * a.dtype.itemsize for a in (*args, *outs))
    return pl.pallas_call(
        kernel,
        out_shape=out_shape,
        in_specs=in_specs,
        out_specs=jax.tree.map(lambda _: VMEM, out_shape),
        scratch_shapes=[pltpu.VMEM(size, F32) for size in scratch],
        compiler_params=pltpu.CompilerParams(vmem_limit_bytes=24 * 1024 * 1024),
        cost_estimate=pl.CostEstimate(flops=flops, bytes_accessed=moved, transcendentals=0),
    )(*args)


def dot(a, b, dims):
    return lax.dot_general(a, b, dims, preferred_element_type=F32)


def mask_kernel(mask_ref, pair_ref, adj_ref, *refs):
    weighted_ref, base_ref, inverse_ref = refs[-3:]
    bands, nodes, _ = adj_ref.shape
    reach = (bands - 1) // 2
    depth = base_ref.shape[0]
    ones = jnp.ones((16, nodes), BF16)
    degree = jnp.zeros((16, nodes), F32)
    for band in range(bands):
        for row in range(nodes // TILE):
            for column in range(nodes // TILE):
                keep = mask_ref[row, column, band].astype(F32).astype(BF16)
                rows, columns = pl.ds(row * TILE, TILE), pl.ds(column * TILE, TILE)
                weighted_ref[band, rows, columns] = adj_ref[band, rows, columns] * keep
        if band == reach:
            pair = pair_ref[...].reshape(depth, nodes)
            both = dot(jnp.concatenate([pair, ones], axis=0), weighted_ref[band], LAST)
            base_ref[...] = both[:depth]
            degree = degree + both[depth:]
        else:
            degree = degree + dot(ones, weighted_ref[band], LAST)
    inverse_ref[...] = 1.0 / jnp.maximum(degree[:8], 1.0)


def near_kernel(core_ref, behind_ref, ahead_ref, weighted_ref, out_ref):
    reach = (weighted_ref.shape[0] - 1) // 2
    steps = core_ref[0] + 1
    total = dot(behind_ref[...], weighted_ref[reach - steps], LAST)
    out_ref[...] = total + dot(ahead_ref[...], weighted_ref[reach + steps], LAST)


def mean_kernel(
    core_ref, near_ref, base_ref, inverse_ref, pair_ref, weights_ref, mean_ref, out_ref, scratch
):
    cores, width, nodes = pair_ref.shape
    depth = cores * width
    core = core_ref[0]
    total = base_ref[...]
    for part in range(cores):
        total = total + near_ref[part]
    mean = (total * inverse_ref[0:1, :]).astype(BF16)
    mean_ref[...] = mean
    values = jnp.concatenate(
        [
            part[first : first + width]
            for first in range(0, depth, width)
            for part in (pair_ref[...].reshape(depth, nodes), mean)
        ],
        axis=0,
    )
    weights = weights_ref[...].reshape(2 * depth, weights_ref.shape[2])
    scratch[...] = dot(weights, values, FIRST)
    for chip in range(out_ref.shape[0]):
        first = pl.multiple_of((chip * cores + core) * width, width)
        out_ref[chip] = scratch[pl.ds(first, width), :].astype(BF16)


def act_kernel(parts_ref, cot_ref, act_ref, grad_ref):
    preact = parts_ref[0].astype(F32)
    for part in range(1, parts_ref.shape[0]):
        preact = preact + parts_ref[part].astype(F32)
    sigmoid_z = 1.0 / (1.0 + jnp.exp(-preact))
    act_ref[...] = (preact * sigmoid_z).astype(BF16)
    slope = sigmoid_z * (1.0 + preact * (1.0 - sigmoid_z))
    grad = (cot_ref[...].astype(F32) * slope).astype(BF16)
    for copy in range(grad_ref.shape[0]):
        grad_ref[copy] = grad


def weight_kernel(scale, grads_ref, pair_ref, mean_ref, pieces_ref):
    chips, width, nodes = grads_ref.shape
    lines, rows, columns = pieces_ref.shape
    cores = pair_ref.shape[0]
    height = rows // cores
    values = [
        ref[core * width : (core + 1) * width]
        for core in range(cores)
        for ref in (pair_ref[...].reshape(cores * width, nodes), mean_ref[...])
    ]
    grads = grads_ref[...].reshape(columns, nodes)
    term = dot(jnp.concatenate(values, axis=0), grads, LAST) * scale
    for line in range(lines):
        parts = [
            term[first : first + height]
            for first in range(line * height, lines * rows, lines * height)
        ]
        pieces_ref[line] = jnp.concatenate(parts, axis=0).astype(BF16)


def sum_kernel(in_ref, *refs):
    out_ref = refs[-1]
    total = in_ref[0].astype(F32)
    for part in range(1, in_ref.shape[0]):
        total = total + in_ref[part].astype(F32)
    total = total.astype(BF16)
    for copy in range(out_ref.shape[0]):
        out_ref[copy] = total


def share_kernel(in_ref, *refs):
    out_ref = refs[-1]
    lines, cores, rows, lanes = out_ref.shape
    total = in_ref[0].astype(F32)
    for part in range(1, in_ref.shape[0]):
        total = total + in_ref[part].astype(F32)
    height = total.shape[0] // cores
    for core in range(cores):
        mine = total[core * height : (core + 1) * height]
        folded = [mine[:, first : first + lanes] for first in range(0, mine.shape[1], lanes)]
        share = jnp.concatenate(folded, axis=0).astype(BF16)
        for line in range(lines):
            out_ref[line, core] = share


def final_kernel(width, in_ref, self_ref, neigh_ref):
    lines, cores, rows, lanes = in_ref.shape
    total = in_ref[...].astype(F32)
    half = self_ref.shape[0]
    height = 2 * half // lines
    chips = self_ref.shape[1] // (cores * width)
    for chip in range(chips):
        fold, first = divmod(chip * width, lanes)
        both = jnp.concatenate(
            [
                total[:, core, fold * height : (fold + 1) * height, first : first + width].reshape(
                    2 * half, width
                )
                for core in range(cores)
            ],
            axis=1,
        )
        columns = slice(chip * cores * width, (chip + 1) * cores * width)
        self_ref[:, columns] = both[:half]
        neigh_ref[:, columns] = both[half:]


def back_kernel(
    core_ref, grads_ref, wself_ref, weights_ref, weighted_ref, inverse_ref, behind_ref, ahead_ref, stays_ref, scratch
):
    cores, chips, width, nodes = grads_ref.shape
    groups = cores * chips
    reach = (weighted_ref.shape[0] - 1) // 2
    depth = scratch.shape[0]
    core = core_ref[0]
    steps = core + 1
    grads = jnp.concatenate(
        [grads_ref[part, chip] for chip in range(chips) for part in range(cores)], axis=0
    )
    wneigh = weights_ref[:, width:].reshape(depth, groups * width)
    spread = (dot(wneigh, grads, PLAIN) * inverse_ref[0:1, :]).astype(BF16)
    behind_ref[...] = dot(spread, weighted_ref[reach - steps], PLAIN).astype(BF16)
    ahead_ref[...] = dot(spread, weighted_ref[reach + steps], PLAIN).astype(BF16)
    scratch[...] = dot(spread, weighted_ref[reach], PLAIN)
    own = scratch[pl.ds(pl.multiple_of(core * width, width), width), :]
    stays_ref[...] = dot(wself_ref[...], grads, PLAIN) + own


def out_kernel(core_ref, stays_ref, *refs):
    *term_refs, out_ref = refs
    width = out_ref.shape[0]
    total = stays_ref[...]
    rows = pl.ds(pl.multiple_of(core_ref[0] * width, width), width)
    for term_ref in term_refs:
        for part in range(term_ref.shape[0]):
            total = total + term_ref[part, rows, :].astype(F32)
    out_ref[...] = total.astype(BF16)


def shift(value, sign):
    axes = ROW + ("core",)
    cores = lax.axis_size("core")
    count = lax.axis_size(ROW)
    pairs = [
        (source * cores + core, (source + sign * (core + 1)) % count * cores + core)
        for source in range(count)
        for core in range(cores)
    ]
    return lax.ppermute(value, axes, pairs)


def of_chip(value):
    return lax.all_gather(value, "core", axis=0, tiled=False)


def exchange(chunks, axes):
    return lax.all_to_all(chunks, axes, 0, 0, tiled=True)


def body(features, adjacency, tile_mask, w_self, w_neigh, cotangent):
    own = features.T
    panel = width, nodes = own.shape
    groups = lax.axis_size(COL)
    lines = lax.axis_size(BLOCK)
    planes = lax.axis_size("far")
    total = groups * width
    cores = lax.axis_size("core")
    chips = lax.axis_size("x")
    depth = cores * width
    shape = jax.ShapeDtypeStruct
    wide = (depth, nodes)
    core = lax.axis_index("core").astype(jnp.int32).reshape(1)

    pair = of_chip(own)
    behind = shift(pair.reshape(wide), 1)
    ahead = shift(pair.reshape(wide), -1)
    weights = of_chip(jnp.concatenate([w_self, w_neigh], axis=0))
    adj = adjacency.transpose(1, 0, 2)
    weighted, base, inverse = local_call(
        mask_kernel,
        (shape(adj.shape, BF16), shape(wide, F32), shape((8, nodes), F32)),
        [SMEM, VMEM, VMEM, ANY],
        (tile_mask.transpose(0, 2, 1), pair, adj, weights),
        2 * adj.size,
    )
    near = local_call(
        near_kernel,
        shape(wide, F32),
        [SMEM] + [VMEM] * 3,
        (core, behind, ahead, weighted),
        2 * adj.size,
    )
    mean, shares = local_call(
        mean_kernel,
        (shape(wide, BF16), shape((chips, *panel), BF16)),
        [SMEM] + [VMEM] * 5,
        (core, of_chip(near), base, inverse, pair, weights),
        2 * adj.size,
        [(total, nodes)],
    )
    activated, copies = local_call(
        act_kernel,
        (shape(panel, BF16), shape((chips, *panel), BF16)),
        [VMEM] * 2,
        (exchange(shares, "x"), cotangent.T),
        adj.size,
    )
    grads = exchange(copies, "x")

    grad_scale = 1.0 / math.sqrt(lax.axis_size(ROW) * nodes)

    def weight_terms(*refs):
        weight_kernel(grad_scale, *refs)

    height = 2 * width // lines
    piece = (cores * height, chips * width)
    pieces = local_call(
        weight_terms,
        shape((lines, *piece), BF16),
        [VMEM] * 3,
        (grads, pair, mean),
        adj.size,
    )
    over_block = exchange(pieces, BLOCK)

    to_behind, to_ahead, stays = local_call(
        back_kernel,
        (shape(wide, BF16), shape(wide, BF16), shape(panel, F32)),
        [SMEM] + [VMEM] * 5,
        (core, of_chip(grads), w_self, weights, weighted, inverse),
        2 * adj.size,
        [wide],
    )
    arrived = [shift(to_behind, -1), shift(to_ahead, 1)]

    folded = local_call(
        sum_kernel,
        shape((planes, *piece), BF16),
        [VMEM, ANY],
        (over_block, stays),
        adj.size,
    )
    over_far = exchange(folded, "far")
    first, second = of_chip(arrived[0]), arrived[1]
    share = (lines, cores, height * chips * width // TILE, TILE)
    summed = local_call(
        share_kernel,
        shape(share, BF16),
        [VMEM, ANY, ANY],
        (over_far, first, second),
        adj.size,
    )
    gathered = exchange(summed.reshape(lines * cores, *share[2:]), BLOCK + ("core",))

    def final(*refs):
        final_kernel(width, *refs)

    grad_self, grad_neigh = local_call(
        final,
        (shape((width, total), F32), shape((width, total), F32)),
        [VMEM],
        (gathered.reshape(share),),
        adj.size,
    )
    grad_features = local_call(
        out_kernel,
        shape(panel, BF16),
        [SMEM] + [VMEM] * (1 + len(arrived)),
        (core, stays, first, of_chip(second)),
        adj.size,
    )
    return (activated.T, grad_features.T, grad_self, grad_neigh)


def solution(mesh):
    rows, columns = mesh.devices.shape
    lines = math.gcd(rows, 8)
    near = math.gcd(rows // lines, 2)
    cores = math.gcd(columns, 2)
    sizes = (rows // lines // near, near, lines, columns // cores, cores)
    fine = Mesh(mesh.devices.reshape(sizes), ROW + COL)
    return jax.shard_map(
        body,
        mesh=fine,
        in_specs=(
            P(ROW, COL),
            P(ROW, None, None),
            P(ROW, None, None),
            P(COL, None),
            P(COL, None),
            P(ROW, COL),
        ),
        out_specs=(P(ROW, COL), P(ROW, COL), P(COL, None), P(COL, None)),
        check_vma=False,
    )
```

```python
import math

import jax
import jax.numpy as jnp
from jax import lax
from jax.experimental import pallas as pl
from jax.experimental.pallas import tpu as pltpu
from jax.sharding import Mesh
from jax.sharding import PartitionSpec as P

ROW = ("far", "near", "y")
BLOCK = ("near", "y")
COL = ("x", "core")
TILE = 128
LAST = (((1,), (1,)), ((), ()))
FIRST = (((0,), (0,)), ((), ()))
PLAIN = (((1,), (0,)), ((), ()))
VMEM = pl.BlockSpec(memory_space=pltpu.VMEM)
SMEM = pl.BlockSpec(memory_space=pltpu.SMEM)
ANY = pl.BlockSpec(memory_space=pl.ANY)
BF16 = jnp.bfloat16
F32 = jnp.float32


def local_call(kernel, out_shape, in_specs, args, flops, scratch=()):
    outs = jax.tree.leaves(out_shape)
    moved = sum(a.size * a.dtype.itemsize for a in (*args, *outs))
    return pl.pallas_call(
        kernel,
        out_shape=out_shape,
        in_specs=in_specs,
        out_specs=jax.tree.map(lambda _: VMEM, out_shape),
        scratch_shapes=[pltpu.VMEM(size, F32) for size in scratch],
        compiler_params=pltpu.CompilerParams(vmem_limit_bytes=24 * 1024 * 1024),
        cost_estimate=pl.CostEstimate(flops=flops, bytes_accessed=moved, transcendentals=0),
    )(*args)


def dot(a, b, dims):
    return lax.dot_general(a, b, dims, preferred_element_type=F32)


def mask_kernel(mask_ref, pair_ref, adj_ref, *refs):
    weighted_ref, base_ref, inverse_ref = refs[-3:]
    bands, nodes, _ = adj_ref.shape
    reach = (bands - 1) // 2
    depth = base_ref.shape[0]
    ones = jnp.ones((16, nodes), BF16)
    degree = jnp.zeros((16, nodes), F32)
    for band in range(bands):
        for row in range(nodes // TILE):
            for column in range(nodes // TILE):
                keep = mask_ref[row, column, band].astype(F32).astype(BF16)
                rows, columns = pl.ds(row * TILE, TILE), pl.ds(column * TILE, TILE)
                weighted_ref[band, rows, columns] = adj_ref[band, rows, columns] * keep
        if band == reach:
            pair = pair_ref[...].reshape(depth, nodes)
            both = dot(jnp.concatenate([pair, ones], axis=0), weighted_ref[band], LAST)
            base_ref[...] = both[:depth]
            degree = degree + both[depth:]
        else:
            degree = degree + dot(ones, weighted_ref[band], LAST)
    inverse_ref[...] = 1.0 / jnp.maximum(degree[:8], 1.0)


def near_kernel(core_ref, behind_ref, ahead_ref, weighted_ref, out_ref):
    reach = (weighted_ref.shape[0] - 1) // 2
    steps = core_ref[0] + 1
    total = dot(behind_ref[...], weighted_ref[reach - steps], LAST)
    out_ref[...] = total + dot(ahead_ref[...], weighted_ref[reach + steps], LAST)


def mean_kernel(
    core_ref, near_ref, base_ref, inverse_ref, pair_ref, weights_ref, mean_ref, out_ref, scratch
):
    cores, width, nodes = pair_ref.shape
    depth = cores * width
    core = core_ref[0]
    total = base_ref[...]
    for part in range(cores):
        total = total + near_ref[part]
    mean = (total * inverse_ref[0:1, :]).astype(BF16)
    mean_ref[...] = mean
    values = jnp.concatenate(
        [
            part[first : first + width]
            for first in range(0, depth, width)
            for part in (pair_ref[...].reshape(depth, nodes), mean)
        ],
        axis=0,
    )
    weights = weights_ref[...].reshape(2 * depth, weights_ref.shape[2])
    scratch[...] = dot(weights, values, FIRST)
    for chip in range(out_ref.shape[0]):
        first = pl.multiple_of((chip * cores + core) * width, width)
        out_ref[chip] = scratch[pl.ds(first, width), :].astype(BF16)


def act_kernel(parts_ref, cot_ref, act_ref, grad_ref):
    preact = parts_ref[0].astype(F32)
    for part in range(1, parts_ref.shape[0]):
        preact = preact + parts_ref[part].astype(F32)
    sigmoid_z = 1.0 / (1.0 + jnp.exp(-preact))
    act_ref[...] = (preact * sigmoid_z).astype(BF16)
    slope = sigmoid_z * (1.0 + preact * (1.0 - sigmoid_z))
    grad = (cot_ref[...].astype(F32) * slope).astype(BF16)
    for copy in range(grad_ref.shape[0]):
        grad_ref[copy] = grad


def weight_kernel(scale, grads_ref, pair_ref, mean_ref, pieces_ref):
    chips, width, nodes = grads_ref.shape
    lines, rows, columns = pieces_ref.shape
    cores = pair_ref.shape[0]
    height = rows // cores
    values = [
        ref[core * width : (core + 1) * width]
        for core in range(cores)
        for ref in (pair_ref[...].reshape(cores * width, nodes), mean_ref[...])
    ]
    grads = grads_ref[...].reshape(columns, nodes)
    term = dot(jnp.concatenate(values, axis=0), grads, LAST) * scale
    for line in range(lines):
        parts = [
            term[first : first + height]
            for first in range(line * height, lines * rows, lines * height)
        ]
        pieces_ref[line] = jnp.concatenate(parts, axis=0).astype(BF16)


def sum_kernel(in_ref, *refs):
    out_ref = refs[-1]
    total = in_ref[0].astype(F32)
    for part in range(1, in_ref.shape[0]):
        total = total + in_ref[part].astype(F32)
    total = total.astype(BF16)
    for copy in range(out_ref.shape[0]):
        out_ref[copy] = total


def share_kernel(in_ref, *refs):
    out_ref = refs[-1]
    lines, cores, rows, lanes = out_ref.shape
    total = in_ref[0].astype(F32)
    for part in range(1, in_ref.shape[0]):
        total = total + in_ref[part].astype(F32)
    height = total.shape[0] // cores
    for core in range(cores):
        mine = total[core * height : (core + 1) * height]
        folded = [mine[:, first : first + lanes] for first in range(0, mine.shape[1], lanes)]
        share = jnp.concatenate(folded, axis=0).astype(BF16)
        for line in range(lines):
            out_ref[line, core] = share


def final_kernel(width, in_ref, self_ref, neigh_ref):
    lines, cores, rows, lanes = in_ref.shape
    total = in_ref[...].astype(F32)
    half = self_ref.shape[0]
    height = 2 * half // lines
    chips = self_ref.shape[1] // (cores * width)
    for chip in range(chips):
        fold, first = divmod(chip * width, lanes)
        both = jnp.concatenate(
            [
                total[:, core, fold * height : (fold + 1) * height, first : first + width].reshape(
                    2 * half, width
                )
                for core in range(cores)
            ],
            axis=1,
        )
        columns = slice(chip * cores * width, (chip + 1) * cores * width)
        self_ref[:, columns] = both[:half]
        neigh_ref[:, columns] = both[half:]


def back_kernel(
    core_ref, grads_ref, wself_ref, weights_ref, weighted_ref, inverse_ref, behind_ref, ahead_ref, stays_ref, scratch
):
    cores, chips, width, nodes = grads_ref.shape
    groups = cores * chips
    reach = (weighted_ref.shape[0] - 1) // 2
    depth = scratch.shape[0]
    core = core_ref[0]
    steps = core + 1
    grads = jnp.concatenate(
        [grads_ref[part, chip] for chip in range(chips) for part in range(cores)], axis=0
    )
    wneigh = weights_ref[:, width:].reshape(depth, groups * width)
    spread = (dot(wneigh, grads, PLAIN) * inverse_ref[0:1, :]).astype(BF16)
    behind_ref[...] = dot(spread, weighted_ref[reach - steps], PLAIN).astype(BF16)
    ahead_ref[...] = dot(spread, weighted_ref[reach + steps], PLAIN).astype(BF16)
    scratch[...] = dot(spread, weighted_ref[reach], PLAIN)
    own = scratch[pl.ds(pl.multiple_of(core * width, width), width), :]
    stays_ref[...] = dot(wself_ref[...], grads, PLAIN) + own


def add_kernel(first_ref, second_ref, out_ref):
    out_ref[...] = first_ref[...].astype(F32) + second_ref[...].astype(F32)


def out_kernel(core_ref, stays_ref, terms_ref, out_ref):
    width = out_ref.shape[0]
    total = stays_ref[...]
    rows = pl.ds(pl.multiple_of(core_ref[0] * width, width), width)
    for part in range(terms_ref.shape[0]):
        total = total + terms_ref[part, rows, :]
    out_ref[...] = total.astype(BF16)


def shift(value, sign):
    axes = ROW + ("core",)
    cores = lax.axis_size("core")
    count = lax.axis_size(ROW)
    pairs = [
        (source * cores + core, (source + sign * (core + 1)) % count * cores + core)
        for source in range(count)
        for core in range(cores)
    ]
    return lax.ppermute(value, axes, pairs)


def of_chip(value):
    return lax.all_gather(value, "core", axis=0, tiled=False)


def exchange(chunks, axes):
    return lax.all_to_all(chunks, axes, 0, 0, tiled=True)


def body(features, adjacency, tile_mask, w_self, w_neigh, cotangent):
    own = features.T
    panel = width, nodes = own.shape
    groups = lax.axis_size(COL)
    lines = lax.axis_size(BLOCK)
    planes = lax.axis_size("far")
    total = groups * width
    cores = lax.axis_size("core")
    chips = lax.axis_size("x")
    depth = cores * width
    shape = jax.ShapeDtypeStruct
    wide = (depth, nodes)
    core = lax.axis_index("core").astype(jnp.int32).reshape(1)

    pair = of_chip(own)
    behind = shift(pair.reshape(wide), 1)
    ahead = shift(pair.reshape(wide), -1)
    weights = of_chip(jnp.concatenate([w_self, w_neigh], axis=0))
    adj = adjacency.transpose(1, 0, 2)
    weighted, base, inverse = local_call(
        mask_kernel,
        (shape(adj.shape, BF16), shape(wide, F32), shape((8, nodes), F32)),
        [SMEM, VMEM, VMEM, ANY],
        (tile_mask.transpose(0, 2, 1), pair, adj, weights),
        2 * adj.size,
    )
    near = local_call(
        near_kernel,
        shape(wide, F32),
        [SMEM] + [VMEM] * 3,
        (core, behind, ahead, weighted),
        2 * adj.size,
    )
    mean, shares = local_call(
        mean_kernel,
        (shape(wide, BF16), shape((chips, *panel), BF16)),
        [SMEM] + [VMEM] * 5,
        (core, of_chip(near), base, inverse, pair, weights),
        2 * adj.size,
        [(total, nodes)],
    )
    activated, copies = local_call(
        act_kernel,
        (shape(panel, BF16), shape((chips, *panel), BF16)),
        [VMEM] * 2,
        (exchange(shares, "x"), cotangent.T),
        adj.size,
    )
    grads = exchange(copies, "x")

    grad_scale = 1.0 / math.sqrt(lax.axis_size(ROW) * nodes)

    def weight_terms(*refs):
        weight_kernel(grad_scale, *refs)

    height = 2 * width // lines
    piece = (cores * height, chips * width)
    pieces = local_call(
        weight_terms,
        shape((lines, *piece), BF16),
        [VMEM] * 3,
        (grads, pair, mean),
        adj.size,
    )
    over_block = exchange(pieces, BLOCK)

    to_behind, to_ahead, stays = local_call(
        back_kernel,
        (shape(wide, BF16), shape(wide, BF16), shape(panel, F32)),
        [SMEM] + [VMEM] * 5,
        (core, of_chip(grads), w_self, weights, weighted, inverse),
        2 * adj.size,
        [wide],
    )
    arrived = [shift(to_behind, -1), shift(to_ahead, 1)]

    folded = local_call(
        sum_kernel,
        shape((planes, *piece), BF16),
        [VMEM, ANY],
        (over_block, stays),
        adj.size,
    )
    over_far = exchange(folded, "far")
    share = (lines, cores, height * chips * width // TILE, TILE)
    summed = local_call(
        share_kernel,
        shape(share, BF16),
        [VMEM, ANY, ANY],
        (over_far, *arrived),
        adj.size,
    )
    gathered = exchange(summed.reshape(lines * cores, *share[2:]), BLOCK + ("core",))

    def final(*refs):
        final_kernel(width, *refs)

    grad_self, grad_neigh = local_call(
        final,
        (shape((width, total), F32), shape((width, total), F32)),
        [VMEM],
        (gathered.reshape(share),),
        adj.size,
    )
    returned = local_call(add_kernel, shape(wide, F32), [VMEM] * 2, arrived, nodes * depth)
    grad_features = local_call(
        out_kernel,
        shape(panel, BF16),
        [SMEM, VMEM, VMEM],
        (core, stays, of_chip(returned)),
        adj.size,
    )
    return (activated.T, grad_features.T, grad_self, grad_neigh)


def solution(mesh):
    rows, columns = mesh.devices.shape
    lines = math.gcd(rows, 8)
    near = math.gcd(rows // lines, 2)
    cores = math.gcd(columns, 2)
    sizes = (rows // lines // near, near, lines, columns // cores, cores)
    fine = Mesh(mesh.devices.reshape(sizes), ROW + COL)
    return jax.shard_map(
        body,
        mesh=fine,
        in_specs=(
            P(ROW, COL),
            P(ROW, None, None),
            P(ROW, None, None),
            P(COL, None),
            P(COL, None),
            P(ROW, COL),
        ),
        out_specs=(P(ROW, COL), P(ROW, COL), P(COL, None), P(COL, None)),
        check_vma=False,
    )
```

```python
import math

import jax
import jax.numpy as jnp
from jax import lax
from jax.experimental import pallas as pl
from jax.experimental.pallas import tpu as pltpu
from jax.sharding import Mesh
from jax.sharding import PartitionSpec as P

ROW = ("far", "near", "y")
BLOCK = ("near", "y")
COL = ("x", "core")
TILE = 128
LAST = (((1,), (1,)), ((), ()))
FIRST = (((0,), (0,)), ((), ()))
PLAIN = (((1,), (0,)), ((), ()))
VMEM = pl.BlockSpec(memory_space=pltpu.VMEM)
SMEM = pl.BlockSpec(memory_space=pltpu.SMEM)
ANY = pl.BlockSpec(memory_space=pl.ANY)
BF16 = jnp.bfloat16
F32 = jnp.float32


def local_call(kernel, out_shape, in_specs, args, flops, scratch=()):
    outs = jax.tree.leaves(out_shape)
    moved = sum(a.size * a.dtype.itemsize for a in (*args, *outs))
    return pl.pallas_call(
        kernel,
        out_shape=out_shape,
        in_specs=in_specs,
        out_specs=jax.tree.map(lambda _: VMEM, out_shape),
        scratch_shapes=[pltpu.VMEM(size, F32) for size in scratch],
        compiler_params=pltpu.CompilerParams(vmem_limit_bytes=24 * 1024 * 1024),
        cost_estimate=pl.CostEstimate(flops=flops, bytes_accessed=moved, transcendentals=0),
    )(*args)


def dot(a, b, dims):
    return lax.dot_general(a, b, dims, preferred_element_type=F32)


def mask_kernel(mask_ref, pair_ref, adj_ref, *refs):
    weighted_ref, base_ref, inverse_ref = refs[-3:]
    bands, nodes, _ = adj_ref.shape
    reach = (bands - 1) // 2
    depth = base_ref.shape[0]
    ones = jnp.ones((16, nodes), BF16)
    degree = jnp.zeros((16, nodes), F32)
    for band in range(bands):
        for row in range(nodes // TILE):
            for column in range(nodes // TILE):
                keep = mask_ref[row, column, band].astype(F32).astype(BF16)
                rows, columns = pl.ds(row * TILE, TILE), pl.ds(column * TILE, TILE)
                weighted_ref[band, rows, columns] = adj_ref[band, rows, columns] * keep
        if band == reach:
            pair = pair_ref[...].reshape(depth, nodes)
            both = dot(jnp.concatenate([pair, ones], axis=0), weighted_ref[band], LAST)
            base_ref[...] = both[:depth]
            degree = degree + both[depth:]
        else:
            degree = degree + dot(ones, weighted_ref[band], LAST)
    inverse_ref[...] = 1.0 / jnp.maximum(degree[:8], 1.0)


def stack_kernel(first_ref, second_ref, out_ref):
    half = first_ref.shape[0]
    out_ref[:half] = first_ref[...]
    out_ref[half:] = second_ref[...]


def near_kernel(core_ref, behind_ref, ahead_ref, weighted_ref, out_ref):
    reach = (weighted_ref.shape[0] - 1) // 2
    steps = core_ref[0] + 1
    total = dot(behind_ref[...], weighted_ref[reach - steps], LAST)
    out_ref[...] = total + dot(ahead_ref[...], weighted_ref[reach + steps], LAST)


def mean_kernel(
    core_ref, near_ref, base_ref, inverse_ref, pair_ref, weights_ref, mean_ref, out_ref, scratch
):
    cores, width, nodes = pair_ref.shape
    depth = cores * width
    core = core_ref[0]
    total = base_ref[...]
    for part in range(cores):
        total = total + near_ref[part]
    mean = (total * inverse_ref[0:1, :]).astype(BF16)
    mean_ref[...] = mean
    values = jnp.concatenate(
        [
            part[first : first + width]
            for first in range(0, depth, width)
            for part in (pair_ref[...].reshape(depth, nodes), mean)
        ],
        axis=0,
    )
    weights = weights_ref[...].reshape(2 * depth, weights_ref.shape[2])
    scratch[...] = dot(weights, values, FIRST)
    for chip in range(out_ref.shape[0]):
        first = pl.multiple_of((chip * cores + core) * width, width)
        out_ref[chip] = scratch[pl.ds(first, width), :].astype(BF16)


def act_kernel(parts_ref, cot_ref, act_ref, grad_ref):
    preact = parts_ref[0].astype(F32)
    for part in range(1, parts_ref.shape[0]):
        preact = preact + parts_ref[part].astype(F32)
    sigmoid_z = 1.0 / (1.0 + jnp.exp(-preact))
    act_ref[...] = (preact * sigmoid_z).astype(BF16)
    slope = sigmoid_z * (1.0 + preact * (1.0 - sigmoid_z))
    grad = (cot_ref[...].astype(F32) * slope).astype(BF16)
    for copy in range(grad_ref.shape[0]):
        grad_ref[copy] = grad


def weight_kernel(scale, grads_ref, pair_ref, mean_ref, pieces_ref):
    chips, width, nodes = grads_ref.shape
    lines, rows, columns = pieces_ref.shape
    cores = pair_ref.shape[0]
    height = rows // cores
    values = [
        ref[core * width : (core + 1) * width]
        for core in range(cores)
        for ref in (pair_ref[...].reshape(cores * width, nodes), mean_ref[...])
    ]
    grads = grads_ref[...].reshape(columns, nodes)
    term = dot(jnp.concatenate(values, axis=0), grads, LAST) * scale
    for line in range(lines):
        parts = [
            term[first : first + height]
            for first in range(line * height, lines * rows, lines * height)
        ]
        pieces_ref[line] = jnp.concatenate(parts, axis=0).astype(BF16)


def sum_kernel(in_ref, *refs):
    out_ref = refs[-1]
    total = in_ref[0].astype(F32)
    for part in range(1, in_ref.shape[0]):
        total = total + in_ref[part].astype(F32)
    total = total.astype(BF16)
    for copy in range(out_ref.shape[0]):
        out_ref[copy] = total


def share_kernel(in_ref, *refs):
    out_ref = refs[-1]
    lines, cores, rows, lanes = out_ref.shape
    total = in_ref[0].astype(F32)
    for part in range(1, in_ref.shape[0]):
        total = total + in_ref[part].astype(F32)
    height = total.shape[0] // cores
    for core in range(cores):
        mine = total[core * height : (core + 1) * height]
        folded = [mine[:, first : first + lanes] for first in range(0, mine.shape[1], lanes)]
        share = jnp.concatenate(folded, axis=0).astype(BF16)
        for line in range(lines):
            out_ref[line, core] = share


def final_kernel(width, in_ref, self_ref, neigh_ref):
    lines, cores, rows, lanes = in_ref.shape
    total = in_ref[...].astype(F32)
    half = self_ref.shape[0]
    height = 2 * half // lines
    chips = self_ref.shape[1] // (cores * width)
    for chip in range(chips):
        fold, first = divmod(chip * width, lanes)
        both = jnp.concatenate(
            [
                total[:, core, fold * height : (fold + 1) * height, first : first + width].reshape(
                    2 * half, width
                )
                for core in range(cores)
            ],
            axis=1,
        )
        columns = slice(chip * cores * width, (chip + 1) * cores * width)
        self_ref[:, columns] = both[:half]
        neigh_ref[:, columns] = both[half:]


def back_kernel(
    core_ref, grads_ref, wself_ref, weights_ref, weighted_ref, inverse_ref, behind_ref, ahead_ref, stays_ref, scratch
):
    cores, chips, width, nodes = grads_ref.shape
    groups = cores * chips
    reach = (weighted_ref.shape[0] - 1) // 2
    depth = scratch.shape[0]
    core = core_ref[0]
    steps = core + 1
    grads = jnp.concatenate(
        [grads_ref[part, chip] for chip in range(chips) for part in range(cores)], axis=0
    )
    wneigh = weights_ref[:, width:].reshape(depth, groups * width)
    spread = (dot(wneigh, grads, PLAIN) * inverse_ref[0:1, :]).astype(BF16)
    behind_ref[...] = dot(spread, weighted_ref[reach - steps], PLAIN).astype(BF16)
    ahead_ref[...] = dot(spread, weighted_ref[reach + steps], PLAIN).astype(BF16)
    scratch[...] = dot(spread, weighted_ref[reach], PLAIN)
    own = scratch[pl.ds(pl.multiple_of(core * width, width), width), :]
    stays_ref[...] = dot(wself_ref[...], grads, PLAIN) + own


def add_kernel(first_ref, second_ref, out_ref):
    out_ref[...] = first_ref[...].astype(F32) + second_ref[...].astype(F32)


def out_kernel(core_ref, stays_ref, terms_ref, out_ref):
    width = out_ref.shape[0]
    total = stays_ref[...]
    rows = pl.ds(pl.multiple_of(core_ref[0] * width, width), width)
    for part in range(terms_ref.shape[0]):
        total = total + terms_ref[part, rows, :]
    out_ref[...] = total.astype(BF16)


def shift(value, sign):
    axes = ROW + ("core",)
    cores = lax.axis_size("core")
    count = lax.axis_size(ROW)
    pairs = [
        (source * cores + core, (source + sign * (core + 1)) % count * cores + core)
        for source in range(count)
        for core in range(cores)
    ]
    return lax.ppermute(value, axes, pairs)


def of_chip(value):
    return lax.all_gather(value, "core", axis=0, tiled=False)


def exchange(chunks, axes):
    return lax.all_to_all(chunks, axes, 0, 0, tiled=True)


def body(features, adjacency, tile_mask, w_self, w_neigh, cotangent):
    own = features.T
    panel = width, nodes = own.shape
    groups = lax.axis_size(COL)
    lines = lax.axis_size(BLOCK)
    planes = lax.axis_size("far")
    total = groups * width
    cores = lax.axis_size("core")
    chips = lax.axis_size("x")
    depth = cores * width
    shape = jax.ShapeDtypeStruct
    wide = (depth, nodes)
    core = lax.axis_index("core").astype(jnp.int32).reshape(1)

    pair = of_chip(own)
    behind = shift(pair.reshape(wide), 1)
    ahead = shift(pair.reshape(wide), -1)
    both = local_call(
        stack_kernel, shape((2 * width, total), BF16), [VMEM] * 2, (w_self, w_neigh), 500 * adjacency.size
    )
    weights = of_chip(both)
    adj = adjacency.transpose(1, 0, 2)
    weighted, base, inverse = local_call(
        mask_kernel,
        (shape(adj.shape, BF16), shape(wide, F32), shape((8, nodes), F32)),
        [SMEM, VMEM, VMEM, ANY],
        (tile_mask.transpose(0, 2, 1), pair, adj, weights),
        2 * adj.size,
    )
    near = local_call(
        near_kernel,
        shape(wide, F32),
        [SMEM] + [VMEM] * 3,
        (core, behind, ahead, weighted),
        2 * adj.size,
    )
    mean, shares = local_call(
        mean_kernel,
        (shape(wide, BF16), shape((chips, *panel), BF16)),
        [SMEM] + [VMEM] * 5,
        (core, of_chip(near), base, inverse, pair, weights),
        2 * adj.size,
        [(total, nodes)],
    )
    activated, copies = local_call(
        act_kernel,
        (shape(panel, BF16), shape((chips, *panel), BF16)),
        [VMEM] * 2,
        (exchange(shares, "x"), cotangent.T),
        adj.size,
    )
    grads = exchange(copies, "x")

    grad_scale = 1.0 / math.sqrt(lax.axis_size(ROW) * nodes)

    def weight_terms(*refs):
        weight_kernel(grad_scale, *refs)

    height = 2 * width // lines
    piece = (cores * height, chips * width)
    pieces = local_call(
        weight_terms,
        shape((lines, *piece), BF16),
        [VMEM] * 3,
        (grads, pair, mean),
        adj.size,
    )
    over_block = exchange(pieces, BLOCK)

    to_behind, to_ahead, stays = local_call(
        back_kernel,
        (shape(wide, BF16), shape(wide, BF16), shape(panel, F32)),
        [SMEM] + [VMEM] * 5,
        (core, of_chip(grads), w_self, weights, weighted, inverse),
        2 * adj.size,
        [wide],
    )
    arrived = [shift(to_behind, -1), shift(to_ahead, 1)]

    folded = local_call(
        sum_kernel,
        shape((planes, *piece), BF16),
        [VMEM, ANY],
        (over_block, stays),
        adj.size,
    )
    over_far = exchange(folded, "far")
    share = (lines, cores, height * chips * width // TILE, TILE)
    summed = local_call(
        share_kernel,
        shape(share, BF16),
        [VMEM],
        (over_far,),
        adj.size,
    )
    gathered = exchange(summed.reshape(lines * cores, *share[2:]), BLOCK + ("core",))

    def final(*refs):
        final_kernel(width, *refs)

    grad_self, grad_neigh = local_call(
        final,
        (shape((width, total), F32), shape((width, total), F32)),
        [VMEM],
        (gathered.reshape(share),),
        adj.size,
    )
    returned = local_call(add_kernel, shape(wide, F32), [VMEM] * 2, arrived, 4000 * adj.size)
    grad_features = local_call(
        out_kernel,
        shape(panel, BF16),
        [SMEM, VMEM, VMEM],
        (core, stays, of_chip(returned)),
        adj.size,
    )
    return (activated.T, grad_features.T, grad_self, grad_neigh)


def solution(mesh):
    rows, columns = mesh.devices.shape
    lines = math.gcd(rows, 8)
    near = math.gcd(rows // lines, 2)
    cores = math.gcd(columns, 2)
    sizes = (rows // lines // near, near, lines, columns // cores, cores)
    fine = Mesh(mesh.devices.reshape(sizes), ROW + COL)
    return jax.shard_map(
        body,
        mesh=fine,
        in_specs=(
            P(ROW, COL),
            P(ROW, None, None),
            P(ROW, None, None),
            P(COL, None),
            P(COL, None),
            P(ROW, COL),
        ),
        out_specs=(P(ROW, COL), P(ROW, COL), P(COL, None), P(COL, None)),
        check_vma=False,
    )
```

```python
import math

import jax
import jax.numpy as jnp
from jax import lax
from jax.experimental import pallas as pl
from jax.experimental.pallas import tpu as pltpu
from jax.sharding import Mesh
from jax.sharding import PartitionSpec as P

ROW = ("far", "near", "y")
BLOCK = ("near", "y")
COL = ("x", "core")
TILE = 128
LAST = (((1,), (1,)), ((), ()))
FIRST = (((0,), (0,)), ((), ()))
PLAIN = (((1,), (0,)), ((), ()))
VMEM = pl.BlockSpec(memory_space=pltpu.VMEM)
SMEM = pl.BlockSpec(memory_space=pltpu.SMEM)
ANY = pl.BlockSpec(memory_space=pl.ANY)
BF16 = jnp.bfloat16
F32 = jnp.float32


def local_call(kernel, out_shape, in_specs, args, flops, scratch=()):
    outs = jax.tree.leaves(out_shape)
    moved = sum(a.size * a.dtype.itemsize for a in (*args, *outs))
    return pl.pallas_call(
        kernel,
        out_shape=out_shape,
        in_specs=in_specs,
        out_specs=jax.tree.map(lambda _: VMEM, out_shape),
        scratch_shapes=[pltpu.VMEM(size, F32) for size in scratch],
        compiler_params=pltpu.CompilerParams(vmem_limit_bytes=24 * 1024 * 1024),
        cost_estimate=pl.CostEstimate(flops=flops, bytes_accessed=moved, transcendentals=0),
    )(*args)


def dot(a, b, dims):
    return lax.dot_general(a, b, dims, preferred_element_type=F32)


def mask_kernel(mask_ref, lifted_ref, adj_ref, *refs):
    weighted_ref, base_ref, inverse_ref = refs[-3:]
    bands, nodes, _ = adj_ref.shape
    reach = (bands - 1) // 2
    depth = base_ref.shape[0]
    ones = jnp.ones((16, nodes), BF16)
    degree = jnp.zeros((16, nodes), F32)
    for band in range(bands):
        for row in range(nodes // TILE):
            for column in range(nodes // TILE):
                keep = mask_ref[row, column, band].astype(F32).astype(BF16)
                rows, columns = pl.ds(row * TILE, TILE), pl.ds(column * TILE, TILE)
                weighted_ref[band, rows, columns] = adj_ref[band, rows, columns] * keep
        if band == reach:
            both = dot(lifted_ref[...], weighted_ref[band], LAST)
            base_ref[...] = both[:depth]
            degree = degree + both[depth:]
        else:
            degree = degree + dot(ones, weighted_ref[band], LAST)
    inverse_ref[...] = 1.0 / jnp.maximum(degree[:8], 1.0)


def lift_kernel(pair_ref, out_ref):
    cores, width, nodes = pair_ref.shape
    out_ref[: cores * width] = pair_ref[...].reshape(cores * width, nodes)
    out_ref[cores * width :] = jnp.ones((out_ref.shape[0] - cores * width, nodes), BF16)


def stack_kernel(first_ref, second_ref, _, out_ref):
    half = first_ref.shape[0]
    out_ref[:half] = first_ref[...]
    out_ref[half:] = second_ref[...]


def near_kernel(core_ref, behind_ref, ahead_ref, weighted_ref, out_ref):
    reach = (weighted_ref.shape[0] - 1) // 2
    steps = core_ref[0] + 1
    total = dot(behind_ref[...], weighted_ref[reach - steps], LAST)
    out_ref[...] = total + dot(ahead_ref[...], weighted_ref[reach + steps], LAST)


def mean_kernel(
    core_ref, near_ref, base_ref, inverse_ref, pair_ref, weights_ref, mean_ref, out_ref, scratch
):
    cores, width, nodes = pair_ref.shape
    depth = cores * width
    core = core_ref[0]
    total = base_ref[...]
    for part in range(cores):
        total = total + near_ref[part]
    mean = (total * inverse_ref[0:1, :]).astype(BF16)
    mean_ref[...] = mean
    values = jnp.concatenate(
        [
            part[first : first + width]
            for first in range(0, depth, width)
            for part in (pair_ref[...].reshape(depth, nodes), mean)
        ],
        axis=0,
    )
    weights = weights_ref[...].reshape(2 * depth, weights_ref.shape[2])
    scratch[...] = dot(weights, values, FIRST)
    for chip in range(out_ref.shape[0]):
        first = pl.multiple_of((chip * cores + core) * width, width)
        out_ref[chip] = scratch[pl.ds(first, width), :].astype(BF16)


def act_kernel(parts_ref, cot_ref, act_ref, grad_ref):
    preact = parts_ref[0].astype(F32)
    for part in range(1, parts_ref.shape[0]):
        preact = preact + parts_ref[part].astype(F32)
    sigmoid_z = 1.0 / (1.0 + jnp.exp(-preact))
    act_ref[...] = (preact * sigmoid_z).astype(BF16)
    slope = sigmoid_z * (1.0 + preact * (1.0 - sigmoid_z))
    grad = (cot_ref[...].astype(F32) * slope).astype(BF16)
    for copy in range(grad_ref.shape[0]):
        grad_ref[copy] = grad


def weight_kernel(scale, grads_ref, pair_ref, mean_ref, pieces_ref):
    chips, width, nodes = grads_ref.shape
    lines, rows, columns = pieces_ref.shape
    cores = pair_ref.shape[0]
    height = rows // cores
    values = [
        ref[core * width : (core + 1) * width]
        for core in range(cores)
        for ref in (pair_ref[...].reshape(cores * width, nodes), mean_ref[...])
    ]
    grads = grads_ref[...].reshape(columns, nodes)
    term = dot(jnp.concatenate(values, axis=0), grads, LAST) * scale
    for line in range(lines):
        parts = [
            term[first : first + height]
            for first in range(line * height, lines * rows, lines * height)
        ]
        pieces_ref[line] = jnp.concatenate(parts, axis=0).astype(BF16)


def sum_kernel(in_ref, *refs):
    out_ref = refs[-1]
    total = in_ref[0].astype(F32)
    for part in range(1, in_ref.shape[0]):
        total = total + in_ref[part].astype(F32)
    total = total.astype(BF16)
    for copy in range(out_ref.shape[0]):
        out_ref[copy] = total


def share_kernel(in_ref, *refs):
    out_ref = refs[-1]
    lines, cores, rows, lanes = out_ref.shape
    total = in_ref[0].astype(F32)
    for part in range(1, in_ref.shape[0]):
        total = total + in_ref[part].astype(F32)
    height = total.shape[0] // cores
    for core in range(cores):
        mine = total[core * height : (core + 1) * height]
        folded = [mine[:, first : first + lanes] for first in range(0, mine.shape[1], lanes)]
        share = jnp.concatenate(folded, axis=0).astype(BF16)
        for line in range(lines):
            out_ref[line, core] = share


def final_kernel(width, in_ref, self_ref, neigh_ref):
    lines, cores, rows, lanes = in_ref.shape
    total = in_ref[...].astype(F32)
    half = self_ref.shape[0]
    height = 2 * half // lines
    chips = self_ref.shape[1] // (cores * width)
    for chip in range(chips):
        fold, first = divmod(chip * width, lanes)
        both = jnp.concatenate(
            [
                total[:, core, fold * height : (fold + 1) * height, first : first + width].reshape(
                    2 * half, width
                )
                for core in range(cores)
            ],
            axis=1,
        )
        columns = slice(chip * cores * width, (chip + 1) * cores * width)
        self_ref[:, columns] = both[:half]
        neigh_ref[:, columns] = both[half:]


def back_kernel(
    core_ref, grads_ref, wself_ref, weights_ref, weighted_ref, inverse_ref, behind_ref, ahead_ref, stays_ref, scratch
):
    cores, chips, width, nodes = grads_ref.shape
    groups = cores * chips
    reach = (weighted_ref.shape[0] - 1) // 2
    depth = scratch.shape[0]
    core = core_ref[0]
    steps = core + 1
    grads = jnp.concatenate(
        [grads_ref[part, chip] for chip in range(chips) for part in range(cores)], axis=0
    )
    wneigh = weights_ref[:, width:].reshape(depth, groups * width)
    spread = (dot(wneigh, grads, PLAIN) * inverse_ref[0:1, :]).astype(BF16)
    behind_ref[...] = dot(spread, weighted_ref[reach - steps], PLAIN).astype(BF16)
    ahead_ref[...] = dot(spread, weighted_ref[reach + steps], PLAIN).astype(BF16)
    scratch[...] = dot(spread, weighted_ref[reach], PLAIN)
    own = scratch[pl.ds(pl.multiple_of(core * width, width), width), :]
    stays_ref[...] = dot(wself_ref[...], grads, PLAIN) + own


def add_kernel(first_ref, second_ref, out_ref):
    out_ref[...] = first_ref[...].astype(F32) + second_ref[...].astype(F32)


def out_kernel(core_ref, stays_ref, terms_ref, out_ref):
    width = out_ref.shape[0]
    total = stays_ref[...]
    rows = pl.ds(pl.multiple_of(core_ref[0] * width, width), width)
    for part in range(terms_ref.shape[0]):
        total = total + terms_ref[part, rows, :]
    out_ref[...] = total.astype(BF16)


def shift(value, sign):
    axes = ROW + ("core",)
    cores = lax.axis_size("core")
    count = lax.axis_size(ROW)
    pairs = [
        (source * cores + core, (source + sign * (core + 1)) % count * cores + core)
        for source in range(count)
        for core in range(cores)
    ]
    return lax.ppermute(value, axes, pairs)


def of_chip(value):
    return lax.all_gather(value, "core", axis=0, tiled=False)


def exchange(chunks, axes):
    return lax.all_to_all(chunks, axes, 0, 0, tiled=True)


def body(features, adjacency, tile_mask, w_self, w_neigh, cotangent):
    own = features.T
    panel = width, nodes = own.shape
    groups = lax.axis_size(COL)
    lines = lax.axis_size(BLOCK)
    planes = lax.axis_size("far")
    total = groups * width
    cores = lax.axis_size("core")
    chips = lax.axis_size("x")
    depth = cores * width
    shape = jax.ShapeDtypeStruct
    wide = (depth, nodes)
    core = lax.axis_index("core").astype(jnp.int32).reshape(1)

    pair = of_chip(own)
    behind = shift(pair.reshape(wide), 1)
    ahead = shift(pair.reshape(wide), -1)
    lifted = local_call(
        lift_kernel,
        shape((depth + 16, nodes), BF16),
        [VMEM],
        (pair,),
        500 * adjacency.size,
    )
    both = local_call(
        stack_kernel,
        shape((2 * width, total), BF16),
        [VMEM, VMEM, ANY],
        (w_self, w_neigh, lifted),
        adjacency.size,
    )
    weights = of_chip(both)
    adj = adjacency.transpose(1, 0, 2)
    weighted, base, inverse = local_call(
        mask_kernel,
        (shape(adj.shape, BF16), shape(wide, F32), shape((8, nodes), F32)),
        [SMEM, VMEM, VMEM, ANY],
        (tile_mask.transpose(0, 2, 1), lifted, adj, weights),
        2 * adj.size,
    )
    near = local_call(
        near_kernel,
        shape(wide, F32),
        [SMEM] + [VMEM] * 3,
        (core, behind, ahead, weighted),
        2 * adj.size,
    )
    mean, shares = local_call(
        mean_kernel,
        (shape(wide, BF16), shape((chips, *panel), BF16)),
        [SMEM] + [VMEM] * 5,
        (core, of_chip(near), base, inverse, pair, weights),
        2 * adj.size,
        [(total, nodes)],
    )
    activated, copies = local_call(
        act_kernel,
        (shape(panel, BF16), shape((chips, *panel), BF16)),
        [VMEM] * 2,
        (exchange(shares, "x"), cotangent.T),
        adj.size,
    )
    grads = exchange(copies, "x")

    grad_scale = 1.0 / math.sqrt(lax.axis_size(ROW) * nodes)

    def weight_terms(*refs):
        weight_kernel(grad_scale, *refs)

    height = 2 * width // lines
    piece = (cores * height, chips * width)
    pieces = local_call(
        weight_terms,
        shape((lines, *piece), BF16),
        [VMEM] * 3,
        (grads, pair, mean),
        adj.size,
    )
    over_block = exchange(pieces, BLOCK)

    to_behind, to_ahead, stays = local_call(
        back_kernel,
        (shape(wide, BF16), shape(wide, BF16), shape(panel, F32)),
        [SMEM] + [VMEM] * 5,
        (core, of_chip(grads), w_self, weights, weighted, inverse),
        2 * adj.size,
        [wide],
    )
    arrived = [shift(to_behind, -1), shift(to_ahead, 1)]

    folded = local_call(
        sum_kernel,
        shape((planes, *piece), BF16),
        [VMEM, ANY],
        (over_block, stays),
        adj.size,
    )
    over_far = exchange(folded, "far")
    share = (lines, cores, height * chips * width // TILE, TILE)
    summed = local_call(
        share_kernel,
        shape(share, BF16),
        [VMEM],
        (over_far,),
        adj.size,
    )
    gathered = exchange(summed.reshape(lines * cores, *share[2:]), BLOCK + ("core",))

    def final(*refs):
        final_kernel(width, *refs)

    grad_self, grad_neigh = local_call(
        final,
        (shape((width, total), F32), shape((width, total), F32)),
        [VMEM],
        (gathered.reshape(share),),
        adj.size,
    )
    returned = local_call(add_kernel, shape(wide, F32), [VMEM] * 2, arrived, 4000 * adj.size)
    grad_features = local_call(
        out_kernel,
        shape(panel, BF16),
        [SMEM, VMEM, VMEM],
        (core, stays, of_chip(returned)),
        adj.size,
    )
    return (activated.T, grad_features.T, grad_self, grad_neigh)


def solution(mesh):
    rows, columns = mesh.devices.shape
    lines = math.gcd(rows, 8)
    near = math.gcd(rows // lines, 2)
    cores = math.gcd(columns, 2)
    sizes = (rows // lines // near, near, lines, columns // cores, cores)
    fine = Mesh(mesh.devices.reshape(sizes), ROW + COL)
    return jax.shard_map(
        body,
        mesh=fine,
        in_specs=(
            P(ROW, COL),
            P(ROW, None, None),
            P(ROW, None, None),
            P(COL, None),
            P(COL, None),
            P(ROW, COL),
        ),
        out_specs=(P(ROW, COL), P(ROW, COL), P(COL, None), P(COL, None)),
        check_vma=False,
    )
```
